256 devices in a mesh: outer: 16 (over y_hi, z), inner: 16 (over y_lo, x, core).
Axes of the slice: x: 4, y: 4 (y_hi: 2, y_lo: 2; y = y_hi * 2 + y_lo), z: 8, core: 2. Of those that a mesh axis runs over, the one named last changes fastest.
Arguments:
- queries: bfloat16 [65536, 2048], P(('outer', 'inner')), may hold values from -64 to 64
- keys: bfloat16 [65536, 2048], P(('outer', 'inner')), may hold values from -6 to 6
- values: bfloat16 [65536, 2048], P(('outer', 'inner')), may hold values from -6 to 6
- level_blocks: int32 [512, 4], P(('outer', 'inner')), may hold values from -1 to 507, as said below
- global_blocks: int32 [8], replicated, may hold values from 0 to 127, as said below
Outputs:
- attended: bfloat16 [65536, 2048], P(('outer', 'inner'))
The draws below stay inside these ranges and needn't reach their ends.
Inputs may be any that keep to these rules, and one draw needn't show every extreme that they name: level_blocks[b, j] is -1 exactly when b // 2 < 2 ** (j + 1); otherwise it is one of the 2 blocks of group b // 2 - 2 ** (j + 1). `global_blocks`: the global summary blocks are distinct.
All inputs are finite; a program needn't handle non-finite values.
Results may differ from the reference program's by a relative error of at most 0.0042.
Values may be sent and summed in bfloat16 or wider, within the bound.
A program may use at most 128 MiB of HBM per device.

```python
import math
import jax
import jax.numpy as jnp
from jax import lax

H = 16
DH = 128
D = 2048
BLK = 128
TOK_DEV = 256
LEV = 4
NGLOB = 8
GROUP_BLOCKS = 2
TOKENS = 65536
NB = 512


def shared_keys(key):
    base_key = jax.random.fold_in(key, 101)
    return jnp.clip(jax.random.normal(base_key, (TOKENS, D), jnp.float32), -6.0, 6.0)


def draw_keys(key, part):
    return shared_keys(key).astype(jnp.bfloat16)


def draw_queries(key, part):
    drawn_rows = jnp.clip(1.5 * jax.random.normal(jax.random.fold_in(key, 202), (TOKENS, D), jnp.float32), -9.0, 9.0)
    return drawn_rows.astype(jnp.bfloat16)


def draw_level_blocks(key, part):
    block_ids = jnp.arange(NB, dtype=jnp.int32)
    group_ids = block_ids // GROUP_BLOCKS
    offsets = jax.random.randint(jax.random.fold_in(key, 303), (NB, LEV), 0, GROUP_BLOCKS, dtype=jnp.int32)
    level_ids = jnp.arange(LEV, dtype=jnp.int32)
    last_top = (block_ids[:, None] == NB - 1) & (level_ids[None, :] == 0)
    offsets = jnp.where(last_top, GROUP_BLOCKS - 1, offsets)
    distances = 2 ** (level_ids + 1)
    source_group = group_ids[:, None] - distances[None, :]
    return jnp.where(source_group >= 0, source_group * GROUP_BLOCKS + offsets, -1).astype(jnp.int32)


def draw_global_blocks(key, part):
    top_block = NB // 4 - 1
    order = jax.random.permutation(jax.random.fold_in(key, 404), top_block)
    chosen = order[:NGLOB - 1].astype(jnp.int32)
    return jnp.concatenate([chosen, jnp.array([top_block], jnp.int32)], axis=0)


def steps_of(key, shape, shards, low, largest):
    gain = 1.0
    for axis_at, parts in shards:
        heights = jax.random.uniform(jax.random.fold_in(jax.random.fold_in(key, 6), axis_at), (parts,), jnp.float32, low / len(shards), largest / len(shards))
        gain = gain * jnp.repeat(jnp.exp(heights), shape[axis_at] // parts).reshape((-1,) + (1,) * (len(shape) - 1 - axis_at))
    return gain


def noise(own_key, dims, spread, reach, cuts=(), kind=jnp.bfloat16):
    values = jax.random.normal(own_key, dims, jnp.float32) * spread
    if len(cuts) > 0:
        values = steps_of(own_key, dims, cuts, -0.22, 0.18) * values
    return jnp.clip(values, min=-reach, max=reach).astype(kind)


def setup_inputs(seed: int = 0) -> dict:
    arg_keys = jax.random.split(jax.random.key(seed), 6)
    queries = draw_queries(jax.random.fold_in(arg_keys[5], 71), 0)
    keys = draw_keys(jax.random.fold_in(arg_keys[5], 71), 0)
    values = noise(arg_keys[2], (TOKENS, D), 1.0, 6.0, ((0, 256),))
    level_blocks = draw_level_blocks(jax.random.fold_in(arg_keys[5], 71), 0)
    global_blocks = draw_global_blocks(jax.random.fold_in(arg_keys[5], 71), 0)
    return dict(queries=queries, keys=keys, values=values, level_blocks=level_blocks, global_blocks=global_blocks)


def reference(queries, keys, values, level_blocks, global_blocks):
    score_scale = 1.0 / math.sqrt(DH)
    zero_rows = jnp.zeros((TOK_DEV, D), keys.dtype)
    padded_keys = jnp.concatenate([zero_rows, keys], axis=0)
    padded_values = jnp.concatenate([zero_rows, values], axis=0)
    key_blocks = keys.reshape(NB, BLK, D)
    value_blocks = values.reshape(NB, BLK, D)
    glob_keys = key_blocks[global_blocks].reshape(NGLOB * BLK, D)
    glob_values = value_blocks[global_blocks].reshape(NGLOB * BLK, D)
    near_offsets = jnp.arange(2 * TOK_DEV, dtype=jnp.int32)
    row_offsets = jnp.arange(BLK, dtype=jnp.int32)
    glob_pos = (global_blocks[:, None] * BLK + row_offsets[None, :]).reshape(NGLOB * BLK).astype(jnp.int32)

    def one_block(block_index):
        group_index = block_index // GROUP_BLOCKS
        group_start = (group_index * TOK_DEV).astype(jnp.int32)
        query_rows = lax.dynamic_slice_in_dim(queries, (block_index * BLK).astype(jnp.int32), BLK, 0)
        near_keys = lax.dynamic_slice_in_dim(padded_keys, group_start, 2 * TOK_DEV, 0)
        near_values = lax.dynamic_slice_in_dim(padded_values, group_start, 2 * TOK_DEV, 0)
        key_pos = group_start - TOK_DEV + near_offsets
        query_pos = block_index * BLK + row_offsets
        near_allowed = (key_pos[None, :] <= query_pos[:, None]) & (key_pos[None, :] >= 0)
        wanted = level_blocks[block_index]
        is_live = wanted >= 0
        slot_index = jnp.where(is_live, wanted, 0)
        level_keys = key_blocks[slot_index].reshape(LEV * BLK, D)
        level_values = value_blocks[slot_index].reshape(LEV * BLK, D)
        level_allowed = jnp.broadcast_to(jnp.repeat(is_live, BLK)[None, :], (BLK, LEV * BLK))
        glob_allowed = glob_pos[None, :] <= query_pos[:, None]
        all_keys = jnp.concatenate([near_keys, level_keys, glob_keys], axis=0)
        all_values = jnp.concatenate([near_values, level_values, glob_values], axis=0)
        allowed = jnp.concatenate([near_allowed, level_allowed, glob_allowed], axis=1)
        query_heads = query_rows.astype(jnp.float32).reshape(BLK, H, DH)
        key_heads = all_keys.astype(jnp.float32).reshape(-1, H, DH)
        value_heads = all_values.astype(jnp.float32).reshape(-1, H, DH)
        scores = jnp.einsum('qhd,khd->hqk', query_heads, key_heads) * score_scale
        scores = jnp.where(allowed[None], scores, -1e+30)
        row_max = lax.optimization_barrier(jnp.max(scores, axis=-1, keepdims=True))
        weights = jnp.exp(scores - row_max)
        row_total = lax.optimization_barrier(jnp.sum(weights, axis=-1, keepdims=True))
        rounded = lax.optimization_barrier(weights.astype(jnp.bfloat16)).astype(jnp.float32)
        summed = jnp.einsum('hqk,khd->qhd', rounded, value_heads)
        result = summed / jnp.transpose(row_total, (1, 0, 2))
        return result.reshape(BLK, D).astype(jnp.bfloat16)
    outputs = lax.map(one_block, jnp.arange(NB, dtype=jnp.int32))
    return outputs.reshape(TOKENS, D)
```

```python
import functools
import math

import jax
import jax.numpy as jnp
from jax import lax
from jax.experimental import pallas as pl
from jax.experimental.pallas import tpu as pltpu
from jax.sharding import PartitionSpec as P

MESH = pl.DeviceIdType.MESH
N = 16
DH = 128
BLK = 128
GRP = 256
LEV = 4
NGLOB = 8
MASKED = -1e30
SCALE_LOG2 = math.log2(math.e) / math.sqrt(DH)


def remote(src, dst, send, recv, device):
    return pltpu.make_async_remote_copy(
        src_ref=src, dst_ref=dst, send_sem=send, recv_sem=recv, device_id=device, device_id_type=MESH
    )


def head_columns(ref, head):
    return ref.at[:, pl.ds(pl.multiple_of(head * DH, DH), DH)]


def dot_keys(rows, keys):
    return lax.dot_general(rows, keys, (((1,), (1,)), ((), ())), preferred_element_type=jnp.float32)


def dot_values(weights, rows):
    return jnp.dot(weights.astype(jnp.bfloat16), rows, preferred_element_type=jnp.float32)


def attend(part, i, qbuf, kv, lbs, gb_ref, gbuf):
    group = part * N + i
    q = qbuf[i]
    row = lax.broadcasted_iota(jnp.int32, (GRP, GRP), 0)
    col = lax.broadcasted_iota(jnp.int32, (GRP, GRP), 1)
    s_prev = jnp.where(group > 0, dot_keys(q, kv[15 + i, 0]), MASKED)
    s_own = jnp.where(col <= row, dot_keys(q, kv[16 + i, 0]), MASKED)
    s_glob = dot_keys(q, gbuf[0:NGLOB].reshape(NGLOB * BLK, DH))
    ahead = (col - row)[:, :BLK]
    s_glob = jnp.concatenate(
        [
            jnp.where(
                ahead <= group * GRP - gb_ref[t] * BLK, s_glob[:, t * BLK : (t + 1) * BLK], MASKED
            )
            for t in range(NGLOB)
        ],
        axis=1,
    )
    s_lev, v_lev = [], []
    for b in range(2):
        keys, vals = [], []
        for j in range(LEV):
            reach = 2 ** (j + 1)
            second = lbs[i, 0, b * LEV + j] == 2 * (group - reach) + 1
            k_pair = kv[16 + i - reach, 0]
            v_pair = kv[16 + i - reach, 1]
            keys.append(jnp.where(second, k_pair[BLK:], k_pair[:BLK]))
            vals.append(jnp.where(second, v_pair[BLK:], v_pair[:BLK]))
        s = dot_keys(q[b * BLK : (b + 1) * BLK], jnp.concatenate(keys, axis=0))
        s_lev.append(
            jnp.concatenate(
                [
                    jnp.where(group >= 2 ** (j + 1), s[:, j * BLK : (j + 1) * BLK], MASKED)
                    for j in range(LEV)
                ],
                axis=1,
            )
        )
        v_lev.append(jnp.concatenate(vals, axis=0))
    s_lev = jnp.concatenate(s_lev, axis=0)
    top = jnp.maximum(
        jnp.maximum(
            jnp.max(s_prev, axis=1, keepdims=True), jnp.max(s_own, axis=1, keepdims=True)
        ),
        jnp.maximum(
            jnp.max(s_glob, axis=1, keepdims=True), jnp.max(s_lev, axis=1, keepdims=True)
        ),
    )
    p_prev = jnp.exp2((s_prev - top) * SCALE_LOG2)
    p_own = jnp.exp2((s_own - top) * SCALE_LOG2)
    p_glob = jnp.exp2((s_glob - top) * SCALE_LOG2)
    p_lev = jnp.exp2((s_lev - top) * SCALE_LOG2)
    total = (
        jnp.sum(p_prev, axis=1, keepdims=True)
        + jnp.sum(p_own, axis=1, keepdims=True)
        + jnp.sum(p_glob, axis=1, keepdims=True)
        + jnp.sum(p_lev, axis=1, keepdims=True)
    )
    acc = (
        dot_values(p_prev, kv[15 + i, 1])
        + dot_values(p_own, kv[16 + i, 1])
        + dot_values(p_glob, gbuf[NGLOB : 2 * NGLOB].reshape(NGLOB * BLK, DH))
        + jnp.concatenate([dot_values(p_lev[:BLK], v_lev[0]), dot_values(p_lev[BLK:], v_lev[1])], axis=0)
    )
    return (acc / total).astype(jnp.bfloat16)


def kernel(
    q_ref, k_ref, v_ref, lb_ref, gb_ref, out_ref,
    qbuf, kv, lbv, lbs, g1src, g1buf, g2src, gbuf, obuf,
    k_send, v_send, q_send, l_send, k_recv, v_recv, q_recv, l_recv,
    h_send, h_recv, g1_send, g1_recv, g2_send, g2_recv, o_send, o_recv, own_sem,
):
    part = lax.axis_index("outer")
    me = lax.axis_index("inner")
    right = lax.rem(part + 1, N)

    barrier = pltpu.get_barrier_semaphore()

    def greet(t, _):
        pl.semaphore_signal(
            barrier, inc=1, device_id=(part, lax.rem(me + t, N)), device_id_type=MESH
        )
        pl.semaphore_signal(
            barrier, inc=1, device_id=(lax.rem(part + t, N), me), device_id_type=MESH
        )
        return 0

    lax.fori_loop(1, N, greet, 0)
    pl.semaphore_wait(barrier, 2 * (N - 1))

    def k_copy(slot, head, device):
        return remote(
            head_columns(k_ref, head), kv.at[16 + slot, 0], k_send.at[head], k_recv.at[slot], device
        )

    def v_copy(slot, head, device):
        return remote(
            head_columns(v_ref, head), kv.at[16 + slot, 1], v_send.at[head], v_recv.at[slot], device
        )

    def q_copy(slot, head, device):
        return remote(
            head_columns(q_ref, head), qbuf.at[slot], q_send.at[head], q_recv.at[slot], device
        )

    def l_copy(slot, head, device):
        return remote(lb_ref, lbv.at[slot], l_send.at[head], l_recv.at[slot], device)

    own_k = pltpu.make_async_copy(head_columns(k_ref, me), kv.at[16 + me, 0], k_recv.at[me])
    own_v = pltpu.make_async_copy(head_columns(v_ref, me), kv.at[16 + me, 1], v_recv.at[me])
    own_q = pltpu.make_async_copy(head_columns(q_ref, me), qbuf.at[me], q_recv.at[me])
    own_l = pltpu.make_async_copy(lb_ref, lbv.at[me], l_recv.at[me])
    own_k.start()
    own_v.start()
    own_q.start()
    own_l.start()

    def send_kv(t, _):
        to = lax.rem(me + t, N)
        k_copy(me, to, (part, to)).start()
        v_copy(me, to, (part, to)).start()
        return 0

    def send_q(t, _):
        to = lax.rem(me + t, N)
        q_copy(me, to, (part, to)).start()
        l_copy(me, to, (part, to)).start()
        return 0

    lax.fori_loop(1, N, send_kv, 0)
    lax.fori_loop(1, N, send_q, 0)

    def halo_copy(slot):
        return remote(
            kv.at[16 + slot], kv.at[slot], h_send.at[slot], h_recv.at[slot], (right, me)
        )

    def forward(n, _):
        slot = lax.rem(8 + n, N)
        k_copy(slot, me, (part, me)).wait_recv()
        v_copy(slot, me, (part, me)).wait_recv()
        halo_copy(slot).start()
        return 0

    lax.fori_loop(0, N, forward, 0)

    def g1_copy(t):
        return remote(g1src.at[t], g1buf.at[part], g1_send.at[t], g1_recv.at[part], (t, me))

    own_g1 = pltpu.make_async_copy(g1src.at[part], g1buf.at[lax.rem(part, 4)], own_sem.at[0])

    @pl.when(part < 4)
    def _():
        for t in range(NGLOB):
            wanted = gb_ref[t] - part * (2 * N)

            def look(slot, found):
                pick_k, pick_v = found
                keys, vals = kv[16 + slot, 0], kv[16 + slot, 1]
                for half in range(2):
                    here = wanted == 2 * slot + half
                    pick_k = jnp.where(here, keys[half * BLK : (half + 1) * BLK], pick_k)
                    pick_v = jnp.where(here, vals[half * BLK : (half + 1) * BLK], pick_v)
                return pick_k, pick_v

            zero = jnp.zeros((BLK, DH), jnp.bfloat16)
            pick_k, pick_v = lax.fori_loop(0, N, look, (zero, zero))
            g1src[2 * t] = pick_k
            g1src[2 * t + 1] = pick_v
        own_g1.start()

        def send_g1(t, _):
            g1_copy_to = lax.rem(part + t, N)
            g1_copy(g1_copy_to).start()
            return 0

        lax.fori_loop(1, N, send_g1, 0)
        own_g1.wait()

    def wait_g1(source, _):
        @pl.when(source != part)
        def _():
            remote(
                g1src.at[0], g1buf.at[source], g1_send.at[0], g1_recv.at[source], (part, me)
            ).wait_recv()

        return 0

    lax.fori_loop(0, 4, wait_g1, 0)
    piece = jnp.zeros((BLK, DH), jnp.bfloat16)
    holder = gb_ref[part // 2] // (2 * N)
    for source in range(4):
        piece = jnp.where(holder == source, g1buf[source], piece)
    g2src[...] = piece

    def g2_place(t):
        return gbuf.at[lax.rem(t, 2) * NGLOB + t // 2]

    def g2_copy(slot, to):
        return remote(g2src, g2_place(slot), g2_send.at[to], g2_recv.at[slot], (to, me))

    own_g2 = pltpu.make_async_copy(g2src, g2_place(part), own_sem.at[1])
    own_g2.start()

    def send_g2(t, _):
        to = lax.rem(part + t, N)
        g2_copy(part, to).start()
        return 0

    lax.fori_loop(1, N, send_g2, 0)

    def wait_q(slot, _):
        q_copy(slot, me, (part, me)).wait_recv()
        l_copy(slot, me, (part, me)).wait_recv()
        return 0

    lax.fori_loop(0, N, wait_q, 0)
    to_scalars = pltpu.make_async_copy(lbv, lbs, own_sem.at[2])
    to_scalars.start()
    to_scalars.wait()

    own_g2.wait()

    def wait_g2(t, _):
        g2_copy(lax.rem(part + t, N), me).wait_recv()
        return 0

    lax.fori_loop(1, N, wait_g2, 0)

    def o_copy(group, head):
        return remote(
            obuf.at[group], head_columns(out_ref, head), o_send.at[group], o_recv.at[head], (part, group)
        )

    own_o = pltpu.make_async_copy(obuf.at[me], head_columns(out_ref, me), own_sem.at[3])

    def step(n, _):
        i = lax.rem(8 + n, N)
        halo_copy(i).wait_recv()
        obuf[i] = attend(part, i, qbuf, kv, lbs, gb_ref, gbuf)

        @pl.when(i == me)
        def _():
            own_o.start()

        @pl.when(i != me)
        def _():
            o_copy(i, me).start()

        return 0

    lax.fori_loop(0, N, step, 0)
    own_o.wait()

    def finish(t, _):
        other = lax.rem(me + t, N)
        k_copy(me, other, (part, other)).wait_send()
        v_copy(me, other, (part, other)).wait_send()
        q_copy(me, other, (part, other)).wait_send()
        l_copy(me, other, (part, other)).wait_send()
        o_copy(other, me).wait_send()
        o_copy(me, other).wait_recv()
        g2_copy(part, lax.rem(part + t, N)).wait_send()
        return 0

    lax.fori_loop(1, N, finish, 0)

    def finish_halo(slot, _):
        halo_copy(slot).wait_send()
        return 0

    lax.fori_loop(0, N, finish_halo, 0)

    @pl.when(part < 4)
    def _():
        def finish_g1(t, _):
            g1_copy(lax.rem(part + t, N)).wait_send()
            return 0

        lax.fori_loop(1, N, finish_g1, 0)


def shards(queries, keys, values, level_blocks, global_blocks):
    rows, width = queries.shape
    levels = jnp.pad(level_blocks.reshape(1, -1), ((0, 7), (0, DH - level_blocks.size)))
    anywhere = pl.BlockSpec(memory_space=pl.ANY)
    sems = pltpu.SemaphoreType.DMA
    return pl.pallas_call(
        kernel,
        out_shape=jax.ShapeDtypeStruct((rows, width), jnp.bfloat16),
        in_specs=[
            anywhere,
            anywhere,
            anywhere,
            pl.BlockSpec(memory_space=pltpu.VMEM),
            pl.BlockSpec(memory_space=pltpu.SMEM),
        ],
        out_specs=anywhere,
        scratch_shapes=[
            pltpu.VMEM((N, GRP, DH), jnp.bfloat16),
            pltpu.VMEM((2 * N, 2, GRP, DH), jnp.bfloat16),
            pltpu.VMEM((N, 8, DH), jnp.int32),
            pltpu.SMEM((N, 8, DH), jnp.int32),
            pltpu.VMEM((N, BLK, DH), jnp.bfloat16),
            pltpu.VMEM((4, BLK, DH), jnp.bfloat16),
            pltpu.VMEM((BLK, DH), jnp.bfloat16),
            pltpu.VMEM((2 * NGLOB, BLK, DH), jnp.bfloat16),
            pltpu.VMEM((N, GRP, DH), jnp.bfloat16),
        ]
        + [sems((N,))] * 8
        + [sems((N,)), sems((N,)), sems((N,)), sems((4,)), sems((N,)), sems((N,)), sems((N,)), sems((N,)), sems((4,))],
        compiler_params=pltpu.CompilerParams(
            collective_id=0, has_side_effects=True, vmem_limit_bytes=40 * 2**20
        ),
        cost_estimate=pl.CostEstimate(
            flops=4 * rows * width * 2048, bytes_accessed=8 * rows * width, transcendentals=rows * 2048 * N
        ),
    )(queries, keys, values, levels, global_blocks)


def solution(mesh):
    placed = P(("outer", "inner"), None)
    return jax.shard_map(
        shards,
        mesh=mesh,
        in_specs=(placed, placed, placed, placed, P()),
        out_specs=placed,
        check_vma=False,
    )
```

```python
import functools
import math

import jax
import jax.numpy as jnp
from jax import lax
from jax.experimental import pallas as pl
from jax.experimental.pallas import tpu as pltpu
from jax.sharding import PartitionSpec as P

MESH = pl.DeviceIdType.MESH
N = 16
DH = 128
BLK = 128
GRP = 256
LEV = 4
NGLOB = 8
MASKED = -1e30
SCALE_LOG2 = math.log2(math.e) / math.sqrt(DH)


def remote(src, dst, send, recv, device):
    return pltpu.make_async_remote_copy(
        src_ref=src, dst_ref=dst, send_sem=send, recv_sem=recv, device_id=device, device_id_type=MESH
    )


def head_columns(ref, head):
    return ref.at[:, pl.ds(pl.multiple_of(head * DH, DH), DH)]


def head_at(part, inner):
    return lax.rem(inner + (part // 8) * 8, N)


def dot_keys(rows, keys):
    return lax.dot_general(rows, keys, (((1,), (1,)), ((), ())), preferred_element_type=jnp.float32)


def dot_values(weights, rows):
    return jnp.dot(weights.astype(jnp.bfloat16), rows, preferred_element_type=jnp.float32)


def attend(part, i, qbuf, kv, lbs, gb_ref, gbuf):
    group = part * N + i
    q = qbuf[i]
    row = lax.broadcasted_iota(jnp.int32, (GRP, GRP), 0)
    col = lax.broadcasted_iota(jnp.int32, (GRP, GRP), 1)
    s_prev = jnp.where(group > 0, dot_keys(q, kv[15 + i, 0]), MASKED)
    s_own = jnp.where(col <= row, dot_keys(q, kv[16 + i, 0]), MASKED)
    s_glob = dot_keys(q, gbuf[0:NGLOB].reshape(NGLOB * BLK, DH))
    ahead = (col - row)[:, :BLK]
    s_glob = jnp.concatenate(
        [
            jnp.where(
                ahead <= group * GRP - gb_ref[t] * BLK, s_glob[:, t * BLK : (t + 1) * BLK], MASKED
            )
            for t in range(NGLOB)
        ],
        axis=1,
    )
    s_lev, v_lev = [], []
    for b in range(2):
        keys, vals = [], []
        for j in range(LEV):
            reach = 2 ** (j + 1)
            second = lbs[i, 0, b * LEV + j] == 2 * (group - reach) + 1
            k_pair = kv[16 + i - reach, 0]
            v_pair = kv[16 + i - reach, 1]
            keys.append(jnp.where(second, k_pair[BLK:], k_pair[:BLK]))
            vals.append(jnp.where(second, v_pair[BLK:], v_pair[:BLK]))
        s = dot_keys(q[b * BLK : (b + 1) * BLK], jnp.concatenate(keys, axis=0))
        s_lev.append(
            jnp.concatenate(
                [
                    jnp.where(group >= 2 ** (j + 1), s[:, j * BLK : (j + 1) * BLK], MASKED)
                    for j in range(LEV)
                ],
                axis=1,
            )
        )
        v_lev.append(jnp.concatenate(vals, axis=0))
    s_lev = jnp.concatenate(s_lev, axis=0)
    top = jnp.maximum(
        jnp.maximum(
            jnp.max(s_prev, axis=1, keepdims=True), jnp.max(s_own, axis=1, keepdims=True)
        ),
        jnp.maximum(
            jnp.max(s_glob, axis=1, keepdims=True), jnp.max(s_lev, axis=1, keepdims=True)
        ),
    )
    p_prev = jnp.exp2((s_prev - top) * SCALE_LOG2)
    p_own = jnp.exp2((s_own - top) * SCALE_LOG2)
    p_glob = jnp.exp2((s_glob - top) * SCALE_LOG2)
    p_lev = jnp.exp2((s_lev - top) * SCALE_LOG2)
    total = (
        jnp.sum(p_prev, axis=1, keepdims=True)
        + jnp.sum(p_own, axis=1, keepdims=True)
        + jnp.sum(p_glob, axis=1, keepdims=True)
        + jnp.sum(p_lev, axis=1, keepdims=True)
    )
    acc = (
        dot_values(p_prev, kv[15 + i, 1])
        + dot_values(p_own, kv[16 + i, 1])
        + dot_values(p_glob, gbuf[NGLOB : 2 * NGLOB].reshape(NGLOB * BLK, DH))
        + jnp.concatenate([dot_values(p_lev[:BLK], v_lev[0]), dot_values(p_lev[BLK:], v_lev[1])], axis=0)
    )
    return (acc / total).astype(jnp.bfloat16)


def kernel(
    q_ref, k_ref, v_ref, lb_ref, gb_ref, out_ref,
    qbuf, kv, lbv, lbs, g1src, g1buf, g2src, gbuf, obuf,
    k_send, v_send, q_send, l_send, k_recv, v_recv, q_recv, l_recv,
    h_send, h_recv, g1_send, g1_recv, g2_send, g2_recv, o_send, o_recv, own_sem,
):
    part = lax.axis_index("outer")
    me = lax.axis_index("inner")
    right = lax.rem(part + 1, N)
    head = head_at(part, me)
    right_inner = head_at(right, head)

    def across(other):
        return (other, head_at(other, head))

    barrier = pltpu.get_barrier_semaphore()

    def greet(t, _):
        pl.semaphore_signal(
            barrier, inc=1, device_id=(part, lax.rem(me + t, N)), device_id_type=MESH
        )
        pl.semaphore_signal(
            barrier, inc=1, device_id=across(lax.rem(part + t, N)), device_id_type=MESH
        )
        return 0

    lax.fori_loop(1, N, greet, 0)
    pl.semaphore_wait(barrier, 2 * (N - 1))

    def k_copy(source, to):
        columns = head_columns(k_ref, head_at(part, to))
        return remote(columns, kv.at[16 + source, 0], k_send.at[to], k_recv.at[source], (part, to))

    def v_copy(source, to):
        columns = head_columns(v_ref, head_at(part, to))
        return remote(columns, kv.at[16 + source, 1], v_send.at[to], v_recv.at[source], (part, to))

    def q_copy(source, to):
        columns = head_columns(q_ref, head_at(part, to))
        return remote(columns, qbuf.at[source], q_send.at[to], q_recv.at[source], (part, to))

    def l_copy(source, to):
        return remote(lb_ref, lbv.at[source], l_send.at[to], l_recv.at[source], (part, to))

    own_k = pltpu.make_async_copy(head_columns(k_ref, head), kv.at[16 + me, 0], k_recv.at[me])
    own_v = pltpu.make_async_copy(head_columns(v_ref, head), kv.at[16 + me, 1], v_recv.at[me])
    own_q = pltpu.make_async_copy(head_columns(q_ref, head), qbuf.at[me], q_recv.at[me])
    own_l = pltpu.make_async_copy(lb_ref, lbv.at[me], l_recv.at[me])
    own_k.start()
    own_v.start()
    own_q.start()
    own_l.start()

    def send_kv(t, _):
        to = lax.rem(me + t, N)
        k_copy(me, to).start()
        v_copy(me, to).start()
        return 0

    lax.fori_loop(1, N, send_kv, 0)

    @pl.when(part == 0)
    def _():
        def blank(slot, _):
            kv[slot] = jnp.zeros((2, GRP, DH), jnp.bfloat16)
            return 0

        lax.fori_loop(0, N, blank, 0)

    def halo_copy(slot):
        return remote(
            kv.at[16 + slot], kv.at[slot], h_send.at[slot], h_recv.at[slot], (right, right_inner)
        )

    own_k.wait()
    own_v.wait()

    @pl.when(part < N - 1)
    def _():
        halo_copy(me).start()

    def forward(t, _):
        slot = lax.rem(me + N - t, N)
        k_copy(slot, me).wait_recv()
        v_copy(slot, me).wait_recv()

        @pl.when(part < N - 1)
        def _():
            halo_copy(slot).start()

        to = lax.rem(me + t, N)
        q_copy(me, to).start()
        l_copy(me, to).start()
        return 0

    lax.fori_loop(1, N, forward, 0)

    def g1_copy(t):
        return remote(g1src.at[t], g1buf.at[part], g1_send.at[t], g1_recv.at[part], across(t))

    own_g1 = pltpu.make_async_copy(g1src.at[part], g1buf.at[lax.rem(part, 4)], own_sem.at[0])

    @pl.when(part < 4)
    def _():
        for t in range(NGLOB):
            wanted = gb_ref[t] - part * (2 * N)

            def look(slot, found):
                pick_k, pick_v = found
                keys, vals = kv[16 + slot, 0], kv[16 + slot, 1]
                for half in range(2):
                    here = wanted == 2 * slot + half
                    pick_k = jnp.where(here, keys[half * BLK : (half + 1) * BLK], pick_k)
                    pick_v = jnp.where(here, vals[half * BLK : (half + 1) * BLK], pick_v)
                return pick_k, pick_v

            zero = jnp.zeros((BLK, DH), jnp.bfloat16)
            pick_k, pick_v = lax.fori_loop(0, N, look, (zero, zero))
            g1src[2 * t] = pick_k
            g1src[2 * t + 1] = pick_v
        own_g1.start()

        def send_g1(t, _):
            g1_copy_to = lax.rem(part + t, N)
            g1_copy(g1_copy_to).start()
            return 0

        lax.fori_loop(1, N, send_g1, 0)
        own_g1.wait()

    def wait_g1(source, _):
        @pl.when(source != part)
        def _():
            remote(
                g1src.at[0], g1buf.at[source], g1_send.at[0], g1_recv.at[source], (part, me)
            ).wait_recv()

        return 0

    lax.fori_loop(0, 4, wait_g1, 0)
    piece = jnp.zeros((BLK, DH), jnp.bfloat16)
    holder = gb_ref[part // 2] // (2 * N)
    for source in range(4):
        piece = jnp.where(holder == source, g1buf[source], piece)
    g2src[...] = piece

    def g2_place(t):
        return gbuf.at[lax.rem(t, 2) * NGLOB + t // 2]

    def g2_copy(slot, to):
        return remote(g2src, g2_place(slot), g2_send.at[to], g2_recv.at[slot], across(to))

    own_g2 = pltpu.make_async_copy(g2src, g2_place(part), own_sem.at[1])
    own_g2.start()

    def send_g2(t, _):
        to = lax.rem(part + t, N)
        g2_copy(part, to).start()
        return 0

    lax.fori_loop(1, N, send_g2, 0)

    own_q.wait()
    own_l.wait()

    def wait_q(t, _):
        slot = lax.rem(me + N - t, N)
        q_copy(slot, me).wait_recv()
        l_copy(slot, me).wait_recv()
        return 0

    lax.fori_loop(1, N, wait_q, 0)
    to_scalars = pltpu.make_async_copy(lbv, lbs, own_sem.at[2])
    to_scalars.start()
    to_scalars.wait()

    own_g2.wait()

    def wait_g2(t, _):
        g2_copy(lax.rem(part + t, N), part).wait_recv()
        return 0

    lax.fori_loop(1, N, wait_g2, 0)

    def o_copy(group, source):
        columns = head_columns(out_ref, head_at(part, source))
        return remote(obuf.at[group], columns, o_send.at[group], o_recv.at[source], (part, group))

    own_o = pltpu.make_async_copy(obuf.at[me], head_columns(out_ref, head), own_sem.at[3])

    first = head_at(lax.rem(part + N - 1, N), head)

    def came(slot):
        return lax.rem(first + N - slot, N)

    def ready(i):
        last = came(i)
        for back in (8, 4, 2, 1):
            other = i + N - back
            last = jnp.maximum(last, jnp.where(other < N, came(lax.rem(other, N)), 0))
        return last

    def step(t, _):
        @pl.when(part > 0)
        def _():
            halo_copy(lax.rem(first + N - t, N)).wait_recv()

        def group(i, _):
            @pl.when(ready(i) == t)
            def _():
                obuf[i] = attend(part, i, qbuf, kv, lbs, gb_ref, gbuf)

                @pl.when(i == me)
                def _():
                    own_o.start()

                @pl.when(i != me)
                def _():
                    o_copy(i, me).start()

            return 0

        lax.fori_loop(0, N, group, 0)
        return 0

    lax.fori_loop(0, N, step, 0)
    own_o.wait()

    def finish(t, _):
        other = lax.rem(me + t, N)
        k_copy(me, other).wait_send()
        v_copy(me, other).wait_send()
        q_copy(me, other).wait_send()
        l_copy(me, other).wait_send()
        o_copy(other, me).wait_send()
        o_copy(me, other).wait_recv()
        g2_copy(part, lax.rem(part + t, N)).wait_send()
        return 0

    lax.fori_loop(1, N, finish, 0)

    @pl.when(part < N - 1)
    def _():
        def finish_halo(slot, _):
            halo_copy(slot).wait_send()
            return 0

        lax.fori_loop(0, N, finish_halo, 0)

    @pl.when(part < 4)
    def _():
        def finish_g1(t, _):
            g1_copy(lax.rem(part + t, N)).wait_send()
            return 0

        lax.fori_loop(1, N, finish_g1, 0)


def shards(queries, keys, values, level_blocks, global_blocks):
    rows, width = queries.shape
    levels = jnp.pad(level_blocks.reshape(1, -1), ((0, 7), (0, DH - level_blocks.size)))
    anywhere = pl.BlockSpec(memory_space=pl.ANY)
    sems = pltpu.SemaphoreType.DMA
    return pl.pallas_call(
        kernel,
        out_shape=jax.ShapeDtypeStruct((rows, width), jnp.bfloat16),
        in_specs=[
            anywhere,
            anywhere,
            anywhere,
            pl.BlockSpec(memory_space=pltpu.VMEM),
            pl.BlockSpec(memory_space=pltpu.SMEM),
        ],
        out_specs=anywhere,
        scratch_shapes=[
            pltpu.VMEM((N, GRP, DH), jnp.bfloat16),
            pltpu.VMEM((2 * N, 2, GRP, DH), jnp.bfloat16),
            pltpu.VMEM((N, 8, DH), jnp.int32),
            pltpu.SMEM((N, 8, DH), jnp.int32),
            pltpu.VMEM((N, BLK, DH), jnp.bfloat16),
            pltpu.VMEM((4, BLK, DH), jnp.bfloat16),
            pltpu.VMEM((BLK, DH), jnp.bfloat16),
            pltpu.VMEM((2 * NGLOB, BLK, DH), jnp.bfloat16),
            pltpu.VMEM((N, GRP, DH), jnp.bfloat16),
        ]
        + [sems((N,))] * 8
        + [sems((N,)), sems((N,)), sems((N,)), sems((4,)), sems((N,)), sems((N,)), sems((N,)), sems((N,)), sems((4,))],
        compiler_params=pltpu.CompilerParams(
            collective_id=0, has_side_effects=True, vmem_limit_bytes=60 * 2**20
        ),
        cost_estimate=pl.CostEstimate(
            flops=4 * rows * width * 2048, bytes_accessed=8 * rows * width, transcendentals=rows * 2048 * N
        ),
    )(queries, keys, values, levels, global_blocks)


def solution(mesh):
    placed = P(("outer", "inner"), None)
    return jax.shard_map(
        shards,
        mesh=mesh,
        in_specs=(placed, placed, placed, placed, P()),
        out_specs=placed,
        check_vma=False,
    )
```

```python
import functools
import math

import jax
import jax.numpy as jnp
from jax import lax
from jax.experimental import pallas as pl
from jax.experimental.pallas import tpu as pltpu
from jax.sharding import PartitionSpec as P

MESH = pl.DeviceIdType.MESH
N = 16
DH = 128
BLK = 128
GRP = 256
LEV = 4
NGLOB = 8
MASKED = -1e30
MOVES = ((2, 0), (1, 0), (3, 1), (0, 0), (2, 1), (1, 1), (3, 0), (0, 1))
HELD = 3
FAR_FIRST = (4, 3, 5, 2, 6, 1, 7)
SCALE_LOG2 = math.log2(math.e) / math.sqrt(DH)


def remote(src, dst, send, recv, device):
    return pltpu.make_async_remote_copy(
        src_ref=src, dst_ref=dst, send_sem=send, recv_sem=recv, device_id=device, device_id_type=MESH
    )


def head_columns(ref, head):
    return ref.at[:, pl.ds(pl.multiple_of(head * DH, DH), DH)]


def head_at(part, inner):
    return lax.rem(inner + (part // 8) * 8, N)


def moved(inner, dy, dx, dc):
    y, x, core = inner // 8, inner // 2, inner
    return lax.rem(y + dy, 2) * 8 + lax.rem(x + dx, 4) * 2 + lax.rem(core + dc, 2)


def dot_keys(rows, keys):
    return lax.dot_general(rows, keys, (((1,), (1,)), ((), ())), preferred_element_type=jnp.float32)


def dot_values(weights, rows):
    return jnp.dot(weights.astype(jnp.bfloat16), rows, preferred_element_type=jnp.float32)


def attend(part, i, masked_far, masked_glob, qbuf, kv, lbs, gb_ref, gbuf):
    group = part * N + i
    q = qbuf[i]
    row = lax.broadcasted_iota(jnp.int32, (GRP, GRP), 0)
    col = lax.broadcasted_iota(jnp.int32, (GRP, GRP), 1)
    s_prev = dot_keys(q, kv[15 + i, 0])
    if masked_far:
        s_prev = jnp.where(group > 0, s_prev, MASKED)
    s_own = jnp.where(col <= row, dot_keys(q, kv[16 + i, 0]), MASKED)
    s_glob = dot_keys(q, gbuf[0:NGLOB].reshape(NGLOB * BLK, DH))
    if masked_glob:
        ahead = (col - row)[:, :BLK]
        s_glob = jnp.concatenate(
            [
                jnp.where(
                    ahead <= group * GRP - gb_ref[t] * BLK, s_glob[:, t * BLK : (t + 1) * BLK], MASKED
                )
                for t in range(NGLOB)
            ],
            axis=1,
        )
    s_lev, v_lev = [], []
    for b in range(2):
        keys, vals = [], []
        for j in range(LEV):
            reach = 2 ** (j + 1)
            second = lbs[i, b, j] == 2 * (group - reach) + 1
            k_pair = kv[16 + i - reach, 0]
            v_pair = kv[16 + i - reach, 1]
            keys.append(jnp.where(second, k_pair[BLK:], k_pair[:BLK]))
            vals.append(jnp.where(second, v_pair[BLK:], v_pair[:BLK]))
        s = dot_keys(q[b * BLK : (b + 1) * BLK], jnp.concatenate(keys, axis=0))
        if masked_far:
            s = jnp.concatenate(
                [
                    jnp.where(group >= 2 ** (j + 1), s[:, j * BLK : (j + 1) * BLK], MASKED)
                    for j in range(LEV)
                ],
                axis=1,
            )
        s_lev.append(s)
        v_lev.append(jnp.concatenate(vals, axis=0))
    s_lev = jnp.concatenate(s_lev, axis=0)
    top = jnp.maximum(
        jnp.maximum(
            jnp.max(s_prev, axis=1, keepdims=True), jnp.max(s_own, axis=1, keepdims=True)
        ),
        jnp.maximum(
            jnp.max(s_glob, axis=1, keepdims=True), jnp.max(s_lev, axis=1, keepdims=True)
        ),
    )
    p_prev = jnp.exp2((s_prev - top) * SCALE_LOG2)
    p_own = jnp.exp2((s_own - top) * SCALE_LOG2)
    p_glob = jnp.exp2((s_glob - top) * SCALE_LOG2)
    p_lev = jnp.exp2((s_lev - top) * SCALE_LOG2)
    total = (
        jnp.sum(p_prev, axis=1, keepdims=True)
        + jnp.sum(p_own, axis=1, keepdims=True)
        + jnp.sum(p_glob, axis=1, keepdims=True)
        + jnp.sum(p_lev, axis=1, keepdims=True)
    )
    acc = (
        dot_values(p_prev, kv[15 + i, 1])
        + dot_values(p_own, kv[16 + i, 1])
        + dot_values(p_glob, gbuf[NGLOB : 2 * NGLOB].reshape(NGLOB * BLK, DH))
        + jnp.concatenate([dot_values(p_lev[:BLK], v_lev[0]), dot_values(p_lev[BLK:], v_lev[1])], axis=0)
    )
    return (acc / total).astype(jnp.bfloat16)


def kernel(
    q_ref, k_ref, v_ref, lb_ref, gb_ref, out_ref,
    qbuf, kv, lbv, lbs, g1src, g1buf, g2src, gbuf, obuf,
    k_send, v_send, q_send, l_send, k_recv, v_recv, q_recv, l_recv,
    h_send, h_recv, g1_send, g1_recv, g2_send, g2_recv, g2_over, o_send, o_recv, own_sem,
):
    part = lax.axis_index("outer")
    me = lax.axis_index("inner")
    right = lax.rem(part + 1, N)
    head = head_at(part, me)
    right_inner = head_at(right, head)

    def across(other):
        return (other, head_at(other, head))

    barrier = pltpu.get_barrier_semaphore()

    def greet(t, _):
        pl.semaphore_signal(
            barrier, inc=1, device_id=(part, lax.rem(me + t, N)), device_id_type=MESH
        )
        pl.semaphore_signal(
            barrier, inc=1, device_id=across(lax.rem(part + t, N)), device_id_type=MESH
        )
        return 0

    lax.fori_loop(1, N, greet, 0)
    pl.semaphore_wait(barrier, 2 * (N - 1))

    def k_copy(source, to):
        columns = head_columns(k_ref, head_at(part, to))
        return remote(columns, kv.at[16 + source, 0], k_send.at[to], k_recv.at[source], (part, to))

    def v_copy(source, to):
        columns = head_columns(v_ref, head_at(part, to))
        return remote(columns, kv.at[16 + source, 1], v_send.at[to], v_recv.at[source], (part, to))

    def q_copy(source, to):
        columns = head_columns(q_ref, head_at(part, to))
        return remote(columns, qbuf.at[source], q_send.at[to], q_recv.at[source], (part, to))

    def l_copy(source, to):
        return remote(lb_ref, lbv.at[source], l_send.at[to], l_recv.at[source], (part, to))

    own_k = pltpu.make_async_copy(head_columns(k_ref, head), kv.at[16 + me, 0], k_recv.at[me])
    own_v = pltpu.make_async_copy(head_columns(v_ref, head), kv.at[16 + me, 1], v_recv.at[me])
    own_q = pltpu.make_async_copy(head_columns(q_ref, head), qbuf.at[me], q_recv.at[me])
    own_l = pltpu.make_async_copy(lb_ref, lbv.at[me], l_recv.at[me])
    own_k.start()
    own_v.start()
    own_q.start()
    own_l.start()

    for dx, dc in MOVES:
        for dy in (1, 0):
            if (dy, dx, dc) != (0, 0, 0):
                to = moved(me, dy, dx, dc)
                k_copy(me, to).start()
                v_copy(me, to).start()

    @pl.when(part == 0)
    def _():
        def blank(slot, _):
            kv[slot] = jnp.zeros((2, GRP, DH), jnp.bfloat16)
            return 0

        lax.fori_loop(0, N, blank, 0)

    def halo_copy(slot):
        return remote(
            kv.at[16 + slot], kv.at[slot], h_send.at[slot], h_recv.at[slot], (right, right_inner)
        )

    own_k.wait()
    own_v.wait()

    def forward(dx, dc):
        @pl.when(part < N - 1)
        def _():
            for dy in (1, 0):
                halo_copy(moved(me, dy, 4 - dx, dc)).start()

    for at, (dx, dc) in enumerate(MOVES):
        for dy in (1, 0):
            if (dy, dx, dc) != (0, 0, 0):
                slot = moved(me, dy, 4 - dx, dc)
                k_copy(slot, me).wait_recv()
                v_copy(slot, me).wait_recv()
                to = moved(me, dy, dx, dc)
                q_copy(me, to).start()
                l_copy(me, to).start()
        if at < len(MOVES) - HELD:
            forward(dx, dc)

    def g1_copy(t):
        return remote(g1src.at[t], g1buf.at[part], g1_send.at[t], g1_recv.at[part], across(t))

    own_g1 = pltpu.make_async_copy(g1src.at[part], g1buf.at[lax.rem(part, 4)], own_sem.at[0])

    @pl.when(part < 4)
    def _():
        for t in range(NGLOB):
            wanted = gb_ref[t] - part * (2 * N)

            def look(slot, found):
                pick_k, pick_v = found
                keys, vals = kv[16 + slot, 0], kv[16 + slot, 1]
                for half in range(2):
                    here = wanted == 2 * slot + half
                    pick_k = jnp.where(here, keys[half * BLK : (half + 1) * BLK], pick_k)
                    pick_v = jnp.where(here, vals[half * BLK : (half + 1) * BLK], pick_v)
                return pick_k, pick_v

            zero = jnp.zeros((BLK, DH), jnp.bfloat16)
            pick_k, pick_v = lax.fori_loop(0, N, look, (zero, zero))
            g1src[2 * t] = pick_k
            g1src[2 * t + 1] = pick_v
        own_g1.start()

        def send_g1(t, _):
            g1_copy_to = lax.rem(part + t, N)
            g1_copy(g1_copy_to).start()
            return 0

        lax.fori_loop(1, N, send_g1, 0)
        own_g1.wait()

    def wait_g1(source, _):
        @pl.when(source != part)
        def _():
            remote(
                g1src.at[0], g1buf.at[source], g1_send.at[0], g1_recv.at[source], (part, me)
            ).wait_recv()

        return 0

    lax.fori_loop(0, 4, wait_g1, 0)
    piece = jnp.zeros((BLK, DH), jnp.bfloat16)
    holder = gb_ref[part // 2] // (2 * N)
    for source in range(4):
        piece = jnp.where(holder == source, g1buf[source], piece)
    g2src[...] = piece

    ring = (part // 8) * 8
    opposite = lax.rem(part + 8, N)

    def g2_place(t):
        return gbuf.at[lax.rem(t, 2) * NGLOB + t // 2]

    def in_ring(step):
        return ring + lax.rem(part + step, 8)

    def g2_copy(slot, to):
        return remote(g2src, g2_place(slot), g2_send.at[to], g2_recv.at[slot], across(to))

    def g2_cross(slot):
        return remote(g2_place(slot), g2_place(slot), g2_over.at[slot], g2_recv.at[slot], across(opposite))

    own_g2 = pltpu.make_async_copy(g2src, g2_place(part), own_sem.at[1])
    own_g2.start()
    for step in FAR_FIRST:
        g2_copy(part, in_ring(step)).start()

    for dx, dc in MOVES[len(MOVES) - HELD :]:
        forward(dx, dc)

    own_g2.wait()
    g2_cross(part).start()
    for step in reversed(FAR_FIRST):
        g2_copy(in_ring(step), part).wait_recv()
        g2_cross(in_ring(step)).start()

    own_q.wait()
    own_l.wait()

    def wait_q(t, _):
        slot = lax.rem(me + N - t, N)
        q_copy(slot, me).wait_recv()
        l_copy(slot, me).wait_recv()
        return 0

    lax.fori_loop(1, N, wait_q, 0)
    to_scalars = pltpu.make_async_copy(lbv, lbs, own_sem.at[2])
    to_scalars.start()
    to_scalars.wait()

    def wait_g2(t, _):
        g2_cross(8 - ring + t).wait_recv()
        return 0

    lax.fori_loop(0, 8, wait_g2, 0)

    def o_copy(group, source):
        columns = head_columns(out_ref, head_at(part, source))
        return remote(obuf.at[group], columns, o_send.at[group], o_recv.at[source], (part, group))

    own_o = pltpu.make_async_copy(obuf.at[me], head_columns(out_ref, head), own_sem.at[3])

    first = head_at(lax.rem(part + N - 1, N), head)

    def groups(masked_far, masked_glob):
        def step(n, _):
            dx = sum(jnp.where(n == at, 4 - move[0], 0) for at, move in enumerate(MOVES))
            dc = sum(jnp.where(n == at, move[1], 0) for at, move in enumerate(MOVES))
            low = moved(first, 0, dx, dc)
            low = jnp.where(low >= 8, low - 8, low)
            pair = n < len(MOVES)

            if not masked_far:

                @pl.when(pair)
                def _():
                    halo_copy(low + 8).wait_recv()
                    halo_copy(low).wait_recv()

            def group(half, _):
                i = jnp.where(
                    pair, low + 8 * (1 - half), lax.rem(me + 2 * (n - len(MOVES)) + half, 4)
                )

                @pl.when((half == 0) | (low >= 4) | (n >= len(MOVES)))
                def _():
                    obuf[i] = attend(part, i, masked_far, masked_glob, qbuf, kv, lbs, gb_ref, gbuf)

                    @pl.when(i == me)
                    def _():
                        own_o.start()

                    @pl.when(i != me)
                    def _():
                        o_copy(i, me).start()

                return 0

            lax.fori_loop(0, 2, group, 0)
            return 0

        lax.fori_loop(0, len(MOVES) + 2, step, 0)

    @pl.when(part == 0)
    def _():
        groups(True, True)

    @pl.when((part > 0) & (part < 4))
    def _():
        groups(False, True)

    @pl.when(part >= 4)
    def _():
        groups(False, False)

    own_o.wait()

    def finish(t, _):
        other = lax.rem(me + t, N)
        k_copy(me, other).wait_send()
        v_copy(me, other).wait_send()
        q_copy(me, other).wait_send()
        l_copy(me, other).wait_send()
        o_copy(other, me).wait_send()
        o_copy(me, other).wait_recv()
        return 0

    lax.fori_loop(1, N, finish, 0)
    g2_cross(part).wait_send()
    for step in FAR_FIRST:
        g2_copy(part, in_ring(step)).wait_send()
        g2_cross(in_ring(step)).wait_send()

    @pl.when(part < N - 1)
    def _():
        def finish_halo(slot, _):
            halo_copy(slot).wait_send()
            return 0

        lax.fori_loop(0, N, finish_halo, 0)

    @pl.when(part < 4)
    def _():
        def finish_g1(t, _):
            g1_copy(lax.rem(part + t, N)).wait_send()
            return 0

        lax.fori_loop(1, N, finish_g1, 0)


def shards(queries, keys, values, level_blocks, global_blocks):
    rows, width = queries.shape
    anywhere = pl.BlockSpec(memory_space=pl.ANY)
    in_place = pl.BlockSpec(memory_space=pltpu.HBM)
    sems = pltpu.SemaphoreType.DMA
    return pl.pallas_call(
        kernel,
        out_shape=jax.ShapeDtypeStruct((rows, width), jnp.bfloat16),
        in_specs=[
            in_place,
            in_place,
            in_place,
            pl.BlockSpec(memory_space=pltpu.VMEM),
            pl.BlockSpec(memory_space=pltpu.SMEM),
        ],
        out_specs=anywhere,
        scratch_shapes=[
            pltpu.VMEM((N, GRP, DH), jnp.bfloat16),
            pltpu.VMEM((2 * N, 2, GRP, DH), jnp.bfloat16),
            pltpu.VMEM((N, 2, LEV), jnp.int32),
            pltpu.SMEM((N, 2, LEV), jnp.int32),
            pltpu.VMEM((N, BLK, DH), jnp.bfloat16),
            pltpu.VMEM((4, BLK, DH), jnp.bfloat16),
            pltpu.VMEM((BLK, DH), jnp.bfloat16),
            pltpu.VMEM((2 * NGLOB, BLK, DH), jnp.bfloat16),
            pltpu.VMEM((N, GRP, DH), jnp.bfloat16),
        ]
        + [sems((N,))] * 8
        + [sems((N,)), sems((N,)), sems((N,)), sems((4,)), sems((N,)), sems((N,)), sems((N,)), sems((N,)), sems((N,)), sems((4,))],
        compiler_params=pltpu.CompilerParams(
            collective_id=0, has_side_effects=True, vmem_limit_bytes=60 * 2**20
        ),
        cost_estimate=pl.CostEstimate(
            flops=4 * rows * width * 2048, bytes_accessed=8 * rows * width, transcendentals=rows * 2048 * N
        ),
    )(queries, keys, values, level_blocks, global_blocks)


def solution(mesh):
    placed = P(("outer", "inner"), None)
    return jax.shard_map(
        shards,
        mesh=mesh,
        in_specs=(placed, placed, placed, placed, P()),
        out_specs=placed,
        check_vma=False,
    )
```

```python
import functools
import math

import jax
import jax.numpy as jnp
from jax import lax
from jax.experimental import pallas as pl
from jax.experimental.pallas import tpu as pltpu
from jax.sharding import PartitionSpec as P

MESH = pl.DeviceIdType.MESH
N = 16
DH = 128
BLK = 128
GRP = 256
LEV = 4
NGLOB = 8
MASKED = -1e30
MOVES = ((2, 0), (1, 0), (3, 1), (0, 0), (2, 1), (1, 1), (3, 0), (0, 1))
HELD = 3
FAR_FIRST = (4, 3, 5, 2, 6, 1, 7)
SCALE_LOG2 = math.log2(math.e) / math.sqrt(DH)


def remote(src, dst, send, recv, device):
    return pltpu.make_async_remote_copy(
        src_ref=src, dst_ref=dst, send_sem=send, recv_sem=recv, device_id=device, device_id_type=MESH
    )


def head_columns(ref, head):
    return ref.at[:, pl.ds(pl.multiple_of(head * DH, DH), DH)]


def head_at(part, inner):
    return lax.rem(inner + (part // 8) * 8, N)


def moved(inner, dy, dx, dc):
    y, x, core = inner // 8, inner // 2, inner
    return lax.rem(y + dy, 2) * 8 + lax.rem(x + dx, 4) * 2 + lax.rem(core + dc, 2)


def dot_keys(rows, keys):
    return lax.dot_general(rows, keys, (((1,), (1,)), ((), ())), preferred_element_type=jnp.float32)


def dot_values(weights, rows):
    return jnp.dot(weights.astype(jnp.bfloat16), rows, preferred_element_type=jnp.float32)


def attend(part, i, masked_far, masked_glob, qbuf, kv, lbs, gb_ref, gbuf):
    group = part * N + i
    q = qbuf[i]
    row = lax.broadcasted_iota(jnp.int32, (GRP, GRP), 0)
    col = lax.broadcasted_iota(jnp.int32, (GRP, GRP), 1)
    s_prev = dot_keys(q, kv[15 + i, 0])
    if masked_far:
        s_prev = jnp.where(group > 0, s_prev, MASKED)
    s_own = jnp.where(col <= row, dot_keys(q, kv[16 + i, 0]), MASKED)
    s_glob = dot_keys(q, gbuf[0:NGLOB].reshape(NGLOB * BLK, DH))
    if masked_glob:
        ahead = (col - row)[:, :BLK]
        s_glob = jnp.concatenate(
            [
                jnp.where(
                    ahead <= group * GRP - gb_ref[t] * BLK, s_glob[:, t * BLK : (t + 1) * BLK], MASKED
                )
                for t in range(NGLOB)
            ],
            axis=1,
        )
    s_lev, v_lev = [], []
    for b in range(2):
        keys, vals = [], []
        for j in range(LEV):
            reach = 2 ** (j + 1)
            second = lbs[i, b, j] == 2 * (group - reach) + 1
            k_pair = kv[16 + i - reach, 0]
            v_pair = kv[16 + i - reach, 1]
            keys.append(jnp.where(second, k_pair[BLK:], k_pair[:BLK]))
            vals.append(jnp.where(second, v_pair[BLK:], v_pair[:BLK]))
        s = dot_keys(q[b * BLK : (b + 1) * BLK], jnp.concatenate(keys, axis=0))
        if masked_far:
            s = jnp.concatenate(
                [
                    jnp.where(group >= 2 ** (j + 1), s[:, j * BLK : (j + 1) * BLK], MASKED)
                    for j in range(LEV)
                ],
                axis=1,
            )
        s_lev.append(s)
        v_lev.append(jnp.concatenate(vals, axis=0))
    s_lev = jnp.concatenate(s_lev, axis=0)
    top = jnp.maximum(
        jnp.maximum(
            jnp.max(s_prev, axis=1, keepdims=True), jnp.max(s_own, axis=1, keepdims=True)
        ),
        jnp.maximum(
            jnp.max(s_glob, axis=1, keepdims=True), jnp.max(s_lev, axis=1, keepdims=True)
        ),
    )
    p_prev = jnp.exp2((s_prev - top) * SCALE_LOG2)
    p_own = jnp.exp2((s_own - top) * SCALE_LOG2)
    p_glob = jnp.exp2((s_glob - top) * SCALE_LOG2)
    p_lev = jnp.exp2((s_lev - top) * SCALE_LOG2)
    total = (
        jnp.sum(p_prev, axis=1, keepdims=True)
        + jnp.sum(p_own, axis=1, keepdims=True)
        + jnp.sum(p_glob, axis=1, keepdims=True)
        + jnp.sum(p_lev, axis=1, keepdims=True)
    )
    acc = (
        dot_values(p_prev, kv[15 + i, 1])
        + dot_values(p_own, kv[16 + i, 1])
        + dot_values(p_glob, gbuf[NGLOB : 2 * NGLOB].reshape(NGLOB * BLK, DH))
        + jnp.concatenate([dot_values(p_lev[:BLK], v_lev[0]), dot_values(p_lev[BLK:], v_lev[1])], axis=0)
    )
    return (acc / total).astype(jnp.bfloat16)


def kernel(
    q_ref, k_ref, v_ref, lb_ref, gb_ref, out_ref,
    qbuf, kv, lbv, lbs, g1src, g1buf, g2src, gbuf, obuf,
    k_send, v_send, q_send, l_send, k_recv, v_recv, q_recv, l_recv,
    h_send, h_recv, g1_send, g1_recv, g2_send, g2_recv, g2_over, o_send, o_recv, own_sem,
):
    part = lax.axis_index("outer")
    me = lax.axis_index("inner")
    right = lax.rem(part + 1, N)
    head = head_at(part, me)
    right_inner = head_at(right, head)

    def across(other):
        return (other, head_at(other, head))

    barrier = pltpu.get_barrier_semaphore()

    def greet(t, _):
        pl.semaphore_signal(
            barrier, inc=1, device_id=(part, lax.rem(me + t, N)), device_id_type=MESH
        )
        pl.semaphore_signal(
            barrier, inc=1, device_id=across(lax.rem(part + t, N)), device_id_type=MESH
        )
        return 0

    lax.fori_loop(1, N, greet, 0)
    pl.semaphore_wait(barrier, 2 * (N - 1))

    def k_copy(source, to):
        columns = head_columns(k_ref, head_at(part, to))
        return remote(columns, kv.at[16 + source, 0], k_send.at[to], k_recv.at[source], (part, to))

    def v_copy(source, to):
        columns = head_columns(v_ref, head_at(part, to))
        return remote(columns, kv.at[16 + source, 1], v_send.at[to], v_recv.at[source], (part, to))

    def q_copy(source, to):
        columns = head_columns(q_ref, head_at(part, to))
        return remote(columns, qbuf.at[source], q_send.at[to], q_recv.at[source], (part, to))

    def l_copy(source, to):
        return remote(lb_ref, lbv.at[source], l_send.at[to], l_recv.at[source], (part, to))

    own_k = pltpu.make_async_copy(head_columns(k_ref, head), kv.at[16 + me, 0], k_recv.at[me])
    own_v = pltpu.make_async_copy(head_columns(v_ref, head), kv.at[16 + me, 1], v_recv.at[me])
    own_q = pltpu.make_async_copy(head_columns(q_ref, head), qbuf.at[me], q_recv.at[me])
    own_l = pltpu.make_async_copy(lb_ref, lbv.at[me], l_recv.at[me])
    own_k.start()
    own_v.start()
    own_q.start()
    own_l.start()

    for dx, dc in MOVES:
        for dy in (1, 0):
            if (dy, dx, dc) != (0, 0, 0):
                to = moved(me, dy, dx, dc)
                k_copy(me, to).start()
                v_copy(me, to).start()

    @pl.when(part == 0)
    def _():
        def blank(slot, _):
            kv[slot] = jnp.zeros((2, GRP, DH), jnp.bfloat16)
            return 0

        lax.fori_loop(0, N, blank, 0)

    def halo_copy(slot):
        return remote(
            kv.at[16 + slot], kv.at[slot], h_send.at[slot], h_recv.at[slot], (right, right_inner)
        )

    own_k.wait()
    own_v.wait()

    def forward(dx, dc):
        @pl.when(part < N - 1)
        def _():
            for dy in (1, 0):
                halo_copy(moved(me, dy, 4 - dx, dc)).start()

    for at, (dx, dc) in enumerate(MOVES):
        for dy in (1, 0):
            if (dy, dx, dc) != (0, 0, 0):
                slot = moved(me, dy, 4 - dx, dc)
                k_copy(slot, me).wait_recv()
                v_copy(slot, me).wait_recv()
                to = moved(me, dy, dx, dc)
                q_copy(me, to).start()
                l_copy(me, to).start()
        if at < len(MOVES) - HELD:
            forward(dx, dc)

    def g1_copy(t):
        return remote(g1src.at[t], g1buf.at[part], g1_send.at[t], g1_recv.at[part], across(t))

    own_g1 = pltpu.make_async_copy(g1src.at[part], g1buf.at[lax.rem(part, 4)], own_sem.at[0])

    @pl.when(part < 4)
    def _():
        for t in range(NGLOB):
            wanted = gb_ref[t] - part * (2 * N)

            def look(slot, found):
                pick_k, pick_v = found
                keys, vals = kv[16 + slot, 0], kv[16 + slot, 1]
                for half in range(2):
                    here = wanted == 2 * slot + half
                    pick_k = jnp.where(here, keys[half * BLK : (half + 1) * BLK], pick_k)
                    pick_v = jnp.where(here, vals[half * BLK : (half + 1) * BLK], pick_v)
                return pick_k, pick_v

            zero = jnp.zeros((BLK, DH), jnp.bfloat16)
            pick_k, pick_v = lax.fori_loop(0, N, look, (zero, zero))
            g1src[2 * t] = pick_k
            g1src[2 * t + 1] = pick_v
        own_g1.start()

        def send_g1(t, _):
            g1_copy_to = lax.rem(part + t, N)
            g1_copy(g1_copy_to).start()
            return 0

        lax.fori_loop(1, N, send_g1, 0)
        own_g1.wait()

    def wait_g1(source, _):
        @pl.when(source != part)
        def _():
            remote(
                g1src.at[0], g1buf.at[source], g1_send.at[0], g1_recv.at[source], (part, me)
            ).wait_recv()

        return 0

    lax.fori_loop(0, 4, wait_g1, 0)
    piece = jnp.zeros((BLK, DH), jnp.bfloat16)
    holder = gb_ref[part // 2] // (2 * N)
    for source in range(4):
        piece = jnp.where(holder == source, g1buf[source], piece)
    g2src[...] = piece

    ring = (part // 8) * 8
    opposite = lax.rem(part + 8, N)

    def g2_place(t):
        return gbuf.at[lax.rem(t, 2) * NGLOB + t // 2]

    def in_ring(step):
        return ring + lax.rem(part + step, 8)

    def g2_copy(slot, to):
        return remote(g2src, g2_place(slot), g2_send.at[to], g2_recv.at[slot], across(to))

    def g2_cross(slot):
        return remote(g2_place(slot), g2_place(slot), g2_over.at[slot], g2_recv.at[slot], across(opposite))

    own_g2 = pltpu.make_async_copy(g2src, g2_place(part), own_sem.at[1])
    own_g2.start()
    for step in FAR_FIRST:
        g2_copy(part, in_ring(step)).start()

    for dx, dc in MOVES[len(MOVES) - HELD :]:
        forward(dx, dc)

    own_g2.wait()
    g2_cross(part).start()
    for step in reversed(FAR_FIRST):
        g2_copy(in_ring(step), part).wait_recv()
        g2_cross(in_ring(step)).start()

    own_q.wait()
    own_l.wait()

    def wait_q(t, _):
        slot = lax.rem(me + N - t, N)
        q_copy(slot, me).wait_recv()
        l_copy(slot, me).wait_recv()
        return 0

    lax.fori_loop(1, N, wait_q, 0)
    to_scalars = pltpu.make_async_copy(lbv, lbs, own_sem.at[2])
    to_scalars.start()
    to_scalars.wait()

    def wait_g2(t, _):
        g2_cross(8 - ring + t).wait_recv()
        return 0

    lax.fori_loop(0, 8, wait_g2, 0)

    def o_copy(group, source):
        columns = head_columns(out_ref, head_at(part, source))
        return remote(obuf.at[group], columns, o_send.at[group], o_recv.at[source], (part, group))

    own_o = pltpu.make_async_copy(obuf.at[me], head_columns(out_ref, head), own_sem.at[3])

    first = head_at(lax.rem(part + N - 1, N), head)

    def pair_low(n):
        dx = sum(jnp.where(n == at, 4 - move[0], 0) for at, move in enumerate(MOVES))
        dc = sum(jnp.where(n == at, move[1], 0) for at, move in enumerate(MOVES))
        low = moved(first, 0, dx, dc)
        return jnp.where(low >= 8, low - 8, low)

    def send_out(i):
        @pl.when(i == me)
        def _():
            own_o.start()

        @pl.when(i != me)
        def _():
            o_copy(i, me).start()

    def groups(masked_far, masked_glob):
        def step(n, _):
            upper = n < 4
            lows = [pair_low(2 * n + k - jnp.where(upper, 0, 8)) for k in range(2)]

            if not masked_far:

                @pl.when(upper)
                def _():
                    for low in lows:
                        halo_copy(low + 8).wait_recv()
                        halo_copy(low).wait_recv()

            two = [low + jnp.where(upper, 8, 0) for low in lows]
            made = [attend(part, i, masked_far, masked_glob, qbuf, kv, lbs, gb_ref, gbuf) for i in two]
            for i, rows in zip(two, made):
                obuf[i] = rows
            for i in two:
                send_out(i)
            return 0

        lax.fori_loop(0, 8, step, 0)

    @pl.when(part == 0)
    def _():
        groups(True, True)

    @pl.when((part > 0) & (part < 4))
    def _():
        groups(False, True)

    @pl.when(part >= 4)
    def _():
        groups(False, False)

    own_o.wait()

    def finish(t, _):
        other = lax.rem(me + t, N)
        k_copy(me, other).wait_send()
        v_copy(me, other).wait_send()
        q_copy(me, other).wait_send()
        l_copy(me, other).wait_send()
        o_copy(other, me).wait_send()
        o_copy(me, other).wait_recv()
        return 0

    lax.fori_loop(1, N, finish, 0)
    g2_cross(part).wait_send()
    for step in FAR_FIRST:
        g2_copy(part, in_ring(step)).wait_send()
        g2_cross(in_ring(step)).wait_send()

    @pl.when(part < N - 1)
    def _():
        def finish_halo(slot, _):
            halo_copy(slot).wait_send()
            return 0

        lax.fori_loop(0, N, finish_halo, 0)

    @pl.when(part < 4)
    def _():
        def finish_g1(t, _):
            g1_copy(lax.rem(part + t, N)).wait_send()
            return 0

        lax.fori_loop(1, N, finish_g1, 0)


def shards(queries, keys, values, level_blocks, global_blocks):
    rows, width = queries.shape
    anywhere = pl.BlockSpec(memory_space=pl.ANY)
    in_place = pl.BlockSpec(memory_space=pltpu.HBM)
    sems = pltpu.SemaphoreType.DMA
    return pl.pallas_call(
        kernel,
        out_shape=jax.ShapeDtypeStruct((rows, width), jnp.bfloat16),
        in_specs=[
            in_place,
            in_place,
            in_place,
            pl.BlockSpec(memory_space=pltpu.VMEM),
            pl.BlockSpec(memory_space=pltpu.SMEM),
        ],
        out_specs=anywhere,
        scratch_shapes=[
            pltpu.VMEM((N, GRP, DH), jnp.bfloat16),
            pltpu.VMEM((2 * N, 2, GRP, DH), jnp.bfloat16),
            pltpu.VMEM((N, 2, LEV), jnp.int32),
            pltpu.SMEM((N, 2, LEV), jnp.int32),
            pltpu.VMEM((N, BLK, DH), jnp.bfloat16),
            pltpu.VMEM((4, BLK, DH), jnp.bfloat16),
            pltpu.VMEM((BLK, DH), jnp.bfloat16),
            pltpu.VMEM((2 * NGLOB, BLK, DH), jnp.bfloat16),
            pltpu.VMEM((N, GRP, DH), jnp.bfloat16),
        ]
        + [sems((N,))] * 8
        + [sems((N,)), sems((N,)), sems((N,)), sems((4,)), sems((N,)), sems((N,)), sems((N,)), sems((N,)), sems((N,)), sems((4,))],
        compiler_params=pltpu.CompilerParams(
            collective_id=0, has_side_effects=True, vmem_limit_bytes=40 * 2**20
        ),
        cost_estimate=pl.CostEstimate(
            flops=4 * rows * width * 2048, bytes_accessed=8 * rows * width, transcendentals=rows * 2048 * N
        ),
    )(
        *[pltpu.with_memory_space_constraint(x, pltpu.HBM) for x in (queries, keys, values)],
        level_blocks,
        global_blocks,
    )


def solution(mesh):
    placed = P(("outer", "inner"), None)
    return jax.shard_map(
        shards,
        mesh=mesh,
        in_specs=(placed, placed, placed, placed, P()),
        out_specs=placed,
        check_vma=False,
    )
```

```python
import functools
import math

import jax
import jax.numpy as jnp
from jax import lax
from jax.experimental import pallas as pl
from jax.experimental.pallas import tpu as pltpu
from jax.sharding import PartitionSpec as P

MESH = pl.DeviceIdType.MESH
N = 16
DH = 128
BLK = 128
GRP = 256
LEV = 4
NGLOB = 8
MASKED = -1e30
MOVES = ((2, 0), (1, 0), (3, 1), (0, 0), (2, 1), (1, 1), (3, 0), (0, 1))
HELD = 3
WINDOW = 3
FAR_FIRST = (4, 3, 5, 2, 6, 1, 7)
SCALE_LOG2 = math.log2(math.e) / math.sqrt(DH)


def remote(src, dst, send, recv, device):
    return pltpu.make_async_remote_copy(
        src_ref=src, dst_ref=dst, send_sem=send, recv_sem=recv, device_id=device, device_id_type=MESH
    )


def head_columns(ref, head):
    return ref.at[:, pl.ds(pl.multiple_of(head * DH, DH), DH)]


def head_at(part, inner):
    return lax.rem(inner + (part // 8) * 8, N)


def moved(inner, dy, dx, dc):
    y, x, core = inner // 8, inner // 2, inner
    return lax.rem(y + dy, 2) * 8 + lax.rem(x + dx, 4) * 2 + lax.rem(core + dc, 2)


def dot_keys(rows, keys):
    return lax.dot_general(rows, keys, (((1,), (1,)), ((), ())), preferred_element_type=jnp.float32)


def dot_values(weights, rows):
    return jnp.dot(weights.astype(jnp.bfloat16), rows, preferred_element_type=jnp.float32)


def attend(part, i, masked_far, masked_glob, qbuf, kv, lbs, gb_ref, gbuf):
    group = part * N + i
    q = qbuf[i]
    row = lax.broadcasted_iota(jnp.int32, (GRP, GRP), 0)
    col = lax.broadcasted_iota(jnp.int32, (GRP, GRP), 1)
    s_prev = dot_keys(q, kv[15 + i, 0])
    if masked_far:
        s_prev = jnp.where(group > 0, s_prev, MASKED)
    s_own = jnp.where(col <= row, dot_keys(q, kv[16 + i, 0]), MASKED)
    s_glob = dot_keys(q, gbuf[0:NGLOB].reshape(NGLOB * BLK, DH))
    if masked_glob:
        ahead = (col - row)[:, :BLK]
        s_glob = jnp.concatenate(
            [
                jnp.where(
                    ahead <= group * GRP - gb_ref[t] * BLK, s_glob[:, t * BLK : (t + 1) * BLK], MASKED
                )
                for t in range(NGLOB)
            ],
            axis=1,
        )
    s_lev, v_lev = [], []
    for b in range(2):
        keys, vals = [], []
        for j in range(LEV):
            reach = 2 ** (j + 1)
            second = lbs[i, b, j] == 2 * (group - reach) + 1
            k_pair = kv[16 + i - reach, 0]
            v_pair = kv[16 + i - reach, 1]
            keys.append(jnp.where(second, k_pair[BLK:], k_pair[:BLK]))
            vals.append(jnp.where(second, v_pair[BLK:], v_pair[:BLK]))
        s = dot_keys(q[b * BLK : (b + 1) * BLK], jnp.concatenate(keys, axis=0))
        if masked_far:
            s = jnp.concatenate(
                [
                    jnp.where(group >= 2 ** (j + 1), s[:, j * BLK : (j + 1) * BLK], MASKED)
                    for j in range(LEV)
                ],
                axis=1,
            )
        s_lev.append(s)
        v_lev.append(jnp.concatenate(vals, axis=0))
    s_lev = jnp.concatenate(s_lev, axis=0)
    top = jnp.maximum(
        jnp.maximum(
            jnp.max(s_prev, axis=1, keepdims=True), jnp.max(s_own, axis=1, keepdims=True)
        ),
        jnp.maximum(
            jnp.max(s_glob, axis=1, keepdims=True), jnp.max(s_lev, axis=1, keepdims=True)
        ),
    )
    p_prev = jnp.exp2((s_prev - top) * SCALE_LOG2)
    p_own = jnp.exp2((s_own - top) * SCALE_LOG2)
    p_glob = jnp.exp2((s_glob - top) * SCALE_LOG2)
    p_lev = jnp.exp2((s_lev - top) * SCALE_LOG2)
    total = (
        jnp.sum(p_prev, axis=1, keepdims=True)
        + jnp.sum(p_own, axis=1, keepdims=True)
        + jnp.sum(p_glob, axis=1, keepdims=True)
        + jnp.sum(p_lev, axis=1, keepdims=True)
    )
    acc = (
        dot_values(p_prev, kv[15 + i, 1])
        + dot_values(p_own, kv[16 + i, 1])
        + dot_values(p_glob, gbuf[NGLOB : 2 * NGLOB].reshape(NGLOB * BLK, DH))
        + jnp.concatenate([dot_values(p_lev[:BLK], v_lev[0]), dot_values(p_lev[BLK:], v_lev[1])], axis=0)
    )
    return (acc / total).astype(jnp.bfloat16)


def kernel(
    q_ref, k_ref, v_ref, lb_ref, gb_ref, out_ref,
    qbuf, kv, lbv, lbs, g1src, g1buf, g2src, gbuf, obuf,
    k_send, v_send, q_send, l_send, k_recv, v_recv, q_recv, l_recv,
    h_send, h_recv, g1_send, g1_recv, g2_send, g2_recv, g2_over, o_send, o_recv, own_sem,
):
    part = lax.axis_index("outer")
    me = lax.axis_index("inner")
    right = lax.rem(part + 1, N)
    head = head_at(part, me)
    right_inner = head_at(right, head)

    def across(other):
        return (other, head_at(other, head))

    barrier = pltpu.get_barrier_semaphore()

    def greet(t, _):
        pl.semaphore_signal(
            barrier, inc=1, device_id=(part, lax.rem(me + t, N)), device_id_type=MESH
        )
        pl.semaphore_signal(
            barrier, inc=1, device_id=across(lax.rem(part + t, N)), device_id_type=MESH
        )
        return 0

    lax.fori_loop(1, N, greet, 0)
    pl.semaphore_wait(barrier, 2 * (N - 1))

    def k_copy(source, to):
        columns = head_columns(k_ref, head_at(part, to))
        return remote(columns, kv.at[16 + source, 0], k_send.at[to], k_recv.at[source], (part, to))

    def v_copy(source, to):
        columns = head_columns(v_ref, head_at(part, to))
        return remote(columns, kv.at[16 + source, 1], v_send.at[to], v_recv.at[source], (part, to))

    def q_copy(source, to):
        columns = head_columns(q_ref, head_at(part, to))
        return remote(columns, qbuf.at[source], q_send.at[to], q_recv.at[source], (part, to))

    def l_copy(source, to):
        return remote(lb_ref, lbv.at[source], l_send.at[to], l_recv.at[source], (part, to))

    own_k = pltpu.make_async_copy(head_columns(k_ref, head), kv.at[16 + me, 0], k_recv.at[me])
    own_v = pltpu.make_async_copy(head_columns(v_ref, head), kv.at[16 + me, 1], v_recv.at[me])
    own_q = pltpu.make_async_copy(head_columns(q_ref, head), qbuf.at[me], q_recv.at[me])
    own_l = pltpu.make_async_copy(lb_ref, lbv.at[me], l_recv.at[me])
    own_k.start()
    own_v.start()
    own_q.start()
    own_l.start()

    def send_pair(dx, dc):
        for dy in (1, 0):
            if (dy, dx, dc) != (0, 0, 0):
                to = moved(me, dy, dx, dc)
                k_copy(me, to).start()
                v_copy(me, to).start()

    for move in MOVES[:WINDOW]:
        send_pair(*move)

    @pl.when(part == 0)
    def _():
        def blank(slot, _):
            kv[slot] = jnp.zeros((2, GRP, DH), jnp.bfloat16)
            return 0

        lax.fori_loop(0, N, blank, 0)

    def halo_copy(slot):
        return remote(
            kv.at[16 + slot], kv.at[slot], h_send.at[slot], h_recv.at[slot], (right, right_inner)
        )

    own_k.wait()
    own_v.wait()

    def forward(dx, dc):
        @pl.when(part < N - 1)
        def _():
            for dy in (1, 0):
                halo_copy(moved(me, dy, 4 - dx, dc)).start()

    for at, (dx, dc) in enumerate(MOVES):
        for dy in (1, 0):
            if (dy, dx, dc) != (0, 0, 0):
                slot = moved(me, dy, 4 - dx, dc)
                k_copy(slot, me).wait_recv()
                v_copy(slot, me).wait_recv()
        if at + WINDOW < len(MOVES):
            send_pair(*MOVES[at + WINDOW])
        if at < len(MOVES) - HELD:
            forward(dx, dc)
        else:
            pl.when(part >= 8)(functools.partial(forward, dx, dc))

    for dx, dc in MOVES:
        for dy in (1, 0):
            if (dy, dx, dc) != (0, 0, 0):
                to = moved(me, dy, dx, dc)
                q_copy(me, to).start()
                l_copy(me, to).start()

    def g1_copy(t):
        return remote(g1src.at[t], g1buf.at[part], g1_send.at[t], g1_recv.at[part], across(t))

    own_g1 = pltpu.make_async_copy(g1src.at[part], g1buf.at[lax.rem(part, 4)], own_sem.at[0])

    @pl.when(part < 4)
    def _():
        for t in range(NGLOB):
            wanted = gb_ref[t] - part * (2 * N)

            def look(slot, found):
                pick_k, pick_v = found
                keys, vals = kv[16 + slot, 0], kv[16 + slot, 1]
                for half in range(2):
                    here = wanted == 2 * slot + half
                    pick_k = jnp.where(here, keys[half * BLK : (half + 1) * BLK], pick_k)
                    pick_v = jnp.where(here, vals[half * BLK : (half + 1) * BLK], pick_v)
                return pick_k, pick_v

            zero = jnp.zeros((BLK, DH), jnp.bfloat16)
            pick_k, pick_v = lax.fori_loop(0, N, look, (zero, zero))
            g1src[2 * t] = pick_k
            g1src[2 * t + 1] = pick_v
        own_g1.start()

        def send_g1(t, _):
            g1_copy_to = lax.rem(part + t, N)
            g1_copy(g1_copy_to).start()
            return 0

        lax.fori_loop(1, N, send_g1, 0)
        own_g1.wait()

    def wait_g1(source, _):
        @pl.when(source != part)
        def _():
            remote(
                g1src.at[0], g1buf.at[source], g1_send.at[0], g1_recv.at[source], (part, me)
            ).wait_recv()

        return 0

    lax.fori_loop(0, 4, wait_g1, 0)
    piece = jnp.zeros((BLK, DH), jnp.bfloat16)
    holder = gb_ref[part // 2] // (2 * N)
    for source in range(4):
        piece = jnp.where(holder == source, g1buf[source], piece)
    g2src[...] = piece

    ring = (part // 8) * 8
    opposite = lax.rem(part + 8, N)

    def g2_place(t):
        return gbuf.at[lax.rem(t, 2) * NGLOB + t // 2]

    def in_ring(step):
        return ring + lax.rem(part + step, 8)

    def g2_copy(slot, to):
        return remote(g2src, g2_place(slot), g2_send.at[to], g2_recv.at[slot], across(to))

    def g2_cross(slot):
        return remote(g2_place(slot), g2_place(slot), g2_over.at[slot], g2_recv.at[slot], across(opposite))

    own_g2 = pltpu.make_async_copy(g2src, g2_place(part), own_sem.at[1])
    own_g2.start()
    for step in FAR_FIRST:
        g2_copy(part, in_ring(step)).start()

    for dx, dc in MOVES[len(MOVES) - HELD :]:
        pl.when(part < 8)(functools.partial(forward, dx, dc))

    own_g2.wait()
    g2_cross(part).start()
    for step in reversed(FAR_FIRST):
        g2_copy(in_ring(step), part).wait_recv()
        g2_cross(in_ring(step)).start()

    own_q.wait()
    own_l.wait()

    def wait_q(t, _):
        slot = lax.rem(me + N - t, N)
        q_copy(slot, me).wait_recv()
        l_copy(slot, me).wait_recv()
        return 0

    lax.fori_loop(1, N, wait_q, 0)
    to_scalars = pltpu.make_async_copy(lbv, lbs, own_sem.at[2])
    to_scalars.start()
    to_scalars.wait()

    def wait_g2(t, _):
        g2_cross(8 - ring + t).wait_recv()
        return 0

    lax.fori_loop(0, 8, wait_g2, 0)

    def o_copy(group, source):
        columns = head_columns(out_ref, head_at(part, source))
        return remote(obuf.at[group], columns, o_send.at[group], o_recv.at[source], (part, group))

    own_o = pltpu.make_async_copy(obuf.at[me], head_columns(out_ref, head), own_sem.at[3])

    first = head_at(lax.rem(part + N - 1, N), head)

    def pair_low(n):
        dx = sum(jnp.where(n == at, 4 - move[0], 0) for at, move in enumerate(MOVES))
        dc = sum(jnp.where(n == at, move[1], 0) for at, move in enumerate(MOVES))
        low = moved(first, 0, dx, dc)
        return jnp.where(low >= 8, low - 8, low)

    def send_out(i):
        @pl.when(i == me)
        def _():
            own_o.start()

        @pl.when(i != me)
        def _():
            o_copy(i, me).start()

    def groups(masked_far, masked_glob):
        def step(n, _):
            upper = n < 4
            lows = [pair_low(2 * n + k - jnp.where(upper, 0, 8)) for k in range(2)]

            if not masked_far:

                @pl.when(upper)
                def _():
                    for low in lows:
                        halo_copy(low + 8).wait_recv()
                        halo_copy(low).wait_recv()

            two = [low + jnp.where(upper, 8, 0) for low in lows]
            made = [attend(part, i, masked_far, masked_glob, qbuf, kv, lbs, gb_ref, gbuf) for i in two]
            for i, rows in zip(two, made):
                obuf[i] = rows
            for i in two:
                send_out(i)
            return 0

        lax.fori_loop(0, 8, step, 0)

    @pl.when(part == 0)
    def _():
        groups(True, True)

    @pl.when((part > 0) & (part < 4))
    def _():
        groups(False, True)

    @pl.when(part >= 4)
    def _():
        groups(False, False)

    own_o.wait()

    def finish(t, _):
        other = lax.rem(me + t, N)
        k_copy(me, other).wait_send()
        v_copy(me, other).wait_send()
        q_copy(me, other).wait_send()
        l_copy(me, other).wait_send()
        o_copy(other, me).wait_send()
        o_copy(me, other).wait_recv()
        return 0

    lax.fori_loop(1, N, finish, 0)
    g2_cross(part).wait_send()
    for step in FAR_FIRST:
        g2_copy(part, in_ring(step)).wait_send()
        g2_cross(in_ring(step)).wait_send()

    @pl.when(part < N - 1)
    def _():
        def finish_halo(slot, _):
            halo_copy(slot).wait_send()
            return 0

        lax.fori_loop(0, N, finish_halo, 0)

    @pl.when(part < 4)
    def _():
        def finish_g1(t, _):
            g1_copy(lax.rem(part + t, N)).wait_send()
            return 0

        lax.fori_loop(1, N, finish_g1, 0)


def shards(queries, keys, values, level_blocks, global_blocks):
    rows, width = queries.shape
    anywhere = pl.BlockSpec(memory_space=pl.ANY)
    in_place = pl.BlockSpec(memory_space=pltpu.HBM)
    sems = pltpu.SemaphoreType.DMA
    return pl.pallas_call(
        kernel,
        out_shape=jax.ShapeDtypeStruct((rows, width), jnp.bfloat16),
        in_specs=[
            in_place,
            in_place,
            in_place,
            pl.BlockSpec(memory_space=pltpu.VMEM),
            pl.BlockSpec(memory_space=pltpu.SMEM),
        ],
        out_specs=anywhere,
        scratch_shapes=[
            pltpu.VMEM((N, GRP, DH), jnp.bfloat16),
            pltpu.VMEM((2 * N, 2, GRP, DH), jnp.bfloat16),
            pltpu.VMEM((N, 2, LEV), jnp.int32),
            pltpu.SMEM((N, 2, LEV), jnp.int32),
            pltpu.VMEM((N, BLK, DH), jnp.bfloat16),
            pltpu.VMEM((4, BLK, DH), jnp.bfloat16),
            pltpu.VMEM((BLK, DH), jnp.bfloat16),
            pltpu.VMEM((2 * NGLOB, BLK, DH), jnp.bfloat16),
            pltpu.VMEM((N, GRP, DH), jnp.bfloat16),
        ]
        + [sems((N,))] * 8
        + [sems((N,)), sems((N,)), sems((N,)), sems((4,)), sems((N,)), sems((N,)), sems((N,)), sems((N,)), sems((N,)), sems((4,))],
        compiler_params=pltpu.CompilerParams(
            collective_id=0, has_side_effects=True, vmem_limit_bytes=40 * 2**20
        ),
        cost_estimate=pl.CostEstimate(
            flops=4 * rows * width * 2048, bytes_accessed=8 * rows * width, transcendentals=rows * 2048 * N
        ),
    )(
        *[pltpu.with_memory_space_constraint(x, pltpu.HBM) for x in (queries, keys, values)],
        level_blocks,
        global_blocks,
    )


def solution(mesh):
    placed = P(("outer", "inner"), None)
    return jax.shard_map(
        shards,
        mesh=mesh,
        in_specs=(placed, placed, placed, placed, P()),
        out_specs=placed,
        check_vma=False,
    )
```

```python
import functools
import math

import jax
import jax.numpy as jnp
from jax import lax
from jax.experimental import pallas as pl
from jax.experimental.pallas import tpu as pltpu
from jax.sharding import PartitionSpec as P

MESH = pl.DeviceIdType.MESH
N = 16
DH = 128
BLK = 128
GRP = 256
LEV = 4
NGLOB = 8
MASKED = -1e30
MOVES = ((2, 0), (1, 0), (3, 1), (0, 0), (2, 1), (1, 1), (3, 0), (0, 1))
HELD = 3
WINDOW = 3
FAR_FIRST = (4, 3, 5, 2, 6, 1, 7)
SCALE_LOG2 = math.log2(math.e) / math.sqrt(DH)


def remote(src, dst, send, recv, device):
    return pltpu.make_async_remote_copy(
        src_ref=src, dst_ref=dst, send_sem=send, recv_sem=recv, device_id=device, device_id_type=MESH
    )


def head_columns(ref, head):
    return ref.at[:, pl.ds(pl.multiple_of(head * DH, DH), DH)]


def head_at(part, inner):
    return lax.rem(inner + (part // 8) * 8, N)


def moved(inner, dy, dx, dc):
    y, x, core = inner // 8, inner // 2, inner
    return lax.rem(y + dy, 2) * 8 + lax.rem(x + dx, 4) * 2 + lax.rem(core + dc, 2)


def dot_keys(rows, keys):
    return lax.dot_general(rows, keys, (((1,), (1,)), ((), ())), preferred_element_type=jnp.float32)


def dot_values(weights, rows):
    return jnp.dot(weights.astype(jnp.bfloat16), rows, preferred_element_type=jnp.float32)


def attend(part, i, masked_far, masked_glob, qbuf, kv, lbs, gb_ref, gbuf):
    group = part * N + i
    q = qbuf[i]
    row = lax.broadcasted_iota(jnp.int32, (GRP, GRP), 0)
    col = lax.broadcasted_iota(jnp.int32, (GRP, GRP), 1)
    s_prev = dot_keys(q, kv[15 + i, 0])
    if masked_far:
        s_prev = jnp.where(group > 0, s_prev, MASKED)
    s_own = jnp.where(col <= row, dot_keys(q, kv[16 + i, 0]), MASKED)
    s_glob = dot_keys(q, gbuf[0:NGLOB].reshape(NGLOB * BLK, DH))
    if masked_glob:
        ahead = (col - row)[:, :BLK]
        s_glob = jnp.concatenate(
            [
                jnp.where(
                    ahead <= group * GRP - gb_ref[t] * BLK, s_glob[:, t * BLK : (t + 1) * BLK], MASKED
                )
                for t in range(NGLOB)
            ],
            axis=1,
        )
    s_lev, v_lev = [], []
    for b in range(2):
        keys, vals = [], []
        for j in range(LEV):
            reach = 2 ** (j + 1)
            second = lbs[i, b, j] == 2 * (group - reach) + 1
            k_pair = kv[16 + i - reach, 0]
            v_pair = kv[16 + i - reach, 1]
            keys.append(jnp.where(second, k_pair[BLK:], k_pair[:BLK]))
            vals.append(jnp.where(second, v_pair[BLK:], v_pair[:BLK]))
        s = dot_keys(q[b * BLK : (b + 1) * BLK], jnp.concatenate(keys, axis=0))
        if masked_far:
            s = jnp.concatenate(
                [
                    jnp.where(group >= 2 ** (j + 1), s[:, j * BLK : (j + 1) * BLK], MASKED)
                    for j in range(LEV)
                ],
                axis=1,
            )
        s_lev.append(s)
        v_lev.append(jnp.concatenate(vals, axis=0))
    s_lev = jnp.concatenate(s_lev, axis=0)
    top = jnp.maximum(
        jnp.maximum(
            jnp.max(s_prev, axis=1, keepdims=True), jnp.max(s_own, axis=1, keepdims=True)
        ),
        jnp.maximum(
            jnp.max(s_glob, axis=1, keepdims=True), jnp.max(s_lev, axis=1, keepdims=True)
        ),
    )
    p_prev = jnp.exp2((s_prev - top) * SCALE_LOG2)
    p_own = jnp.exp2((s_own - top) * SCALE_LOG2)
    p_glob = jnp.exp2((s_glob - top) * SCALE_LOG2)
    p_lev = jnp.exp2((s_lev - top) * SCALE_LOG2)
    total = (
        jnp.sum(p_prev, axis=1, keepdims=True)
        + jnp.sum(p_own, axis=1, keepdims=True)
        + jnp.sum(p_glob, axis=1, keepdims=True)
        + jnp.sum(p_lev, axis=1, keepdims=True)
    )
    acc = (
        dot_values(p_prev, kv[15 + i, 1])
        + dot_values(p_own, kv[16 + i, 1])
        + dot_values(p_glob, gbuf[NGLOB : 2 * NGLOB].reshape(NGLOB * BLK, DH))
        + jnp.concatenate([dot_values(p_lev[:BLK], v_lev[0]), dot_values(p_lev[BLK:], v_lev[1])], axis=0)
    )
    return (acc / total).astype(jnp.bfloat16)


def kernel(
    q_ref, k_ref, v_ref, lb_ref, gb_ref, out_ref,
    qbuf, kv, lbv, lbs, g1src, g1buf, g2src, gbuf, obuf,
    k_send, v_send, q_send, l_send, k_recv, v_recv, q_recv, l_recv,
    h_send, h_recv, g1_send, g1_recv, g2_send, g2_recv, g2_over, o_send, o_recv, own_sem,
):
    part = lax.axis_index("outer")
    me = lax.axis_index("inner")
    right = lax.rem(part + 1, N)
    head = head_at(part, me)
    right_inner = head_at(right, head)

    def across(other):
        return (other, head_at(other, head))

    barrier = pltpu.get_barrier_semaphore()

    def greet(t, _):
        pl.semaphore_signal(
            barrier, inc=1, device_id=(part, lax.rem(me + t, N)), device_id_type=MESH
        )
        pl.semaphore_signal(
            barrier, inc=1, device_id=across(lax.rem(part + t, N)), device_id_type=MESH
        )
        return 0

    lax.fori_loop(1, N, greet, 0)
    pl.semaphore_wait(barrier, 2 * (N - 1))

    def k_copy(source, to):
        columns = head_columns(k_ref, head_at(part, to))
        return remote(columns, kv.at[16 + source, 0], k_send.at[to], k_recv.at[source], (part, to))

    def v_copy(source, to):
        columns = head_columns(v_ref, head_at(part, to))
        return remote(columns, kv.at[16 + source, 1], v_send.at[to], v_recv.at[source], (part, to))

    def q_copy(source, to):
        columns = head_columns(q_ref, head_at(part, to))
        return remote(columns, qbuf.at[source], q_send.at[to], q_recv.at[source], (part, to))

    def l_copy(source, to):
        return remote(lb_ref, lbv.at[source], l_send.at[to], l_recv.at[source], (part, to))

    own_k = pltpu.make_async_copy(head_columns(k_ref, head), kv.at[16 + me, 0], k_recv.at[me])
    own_v = pltpu.make_async_copy(head_columns(v_ref, head), kv.at[16 + me, 1], v_recv.at[me])
    own_q = pltpu.make_async_copy(head_columns(q_ref, head), qbuf.at[me], q_recv.at[me])
    own_l = pltpu.make_async_copy(lb_ref, lbv.at[me], l_recv.at[me])
    own_k.start()
    own_v.start()
    own_q.start()
    own_l.start()

    def send_pair(dx, dc):
        for dy in (1, 0):
            if (dy, dx, dc) != (0, 0, 0):
                to = moved(me, dy, dx, dc)
                k_copy(me, to).start()
                v_copy(me, to).start()

    for move in MOVES[:WINDOW]:
        send_pair(*move)

    @pl.when(part == 0)
    def _():
        def blank(slot, _):
            kv[slot] = jnp.zeros((2, GRP, DH), jnp.bfloat16)
            return 0

        lax.fori_loop(0, N, blank, 0)

    def halo_copy(slot):
        return remote(
            kv.at[16 + slot], kv.at[slot], h_send.at[slot], h_recv.at[slot], (right, right_inner)
        )

    own_k.wait()
    own_v.wait()

    def forward(dx, dc):
        @pl.when(part < N - 1)
        def _():
            for dy in (1, 0):
                halo_copy(moved(me, dy, 4 - dx, dc)).start()

    for at, (dx, dc) in enumerate(MOVES):
        for dy in (1, 0):
            if (dy, dx, dc) != (0, 0, 0):
                slot = moved(me, dy, 4 - dx, dc)
                k_copy(slot, me).wait_recv()
                v_copy(slot, me).wait_recv()
        if at + WINDOW < len(MOVES):
            send_pair(*MOVES[at + WINDOW])
        if at < len(MOVES) - HELD:
            forward(dx, dc)
        else:
            pl.when(part >= 8)(functools.partial(forward, dx, dc))

    for dx, dc in MOVES:
        for dy in (1, 0):
            if (dy, dx, dc) != (0, 0, 0):
                to = moved(me, dy, dx, dc)
                q_copy(me, to).start()
                l_copy(me, to).start()

    def g1_copy(t):
        return remote(g1src.at[t], g1buf.at[part], g1_send.at[t], g1_recv.at[part], across(t))

    own_g1 = pltpu.make_async_copy(g1src.at[part], g1buf.at[lax.rem(part, 4)], own_sem.at[0])

    @pl.when(part < 4)
    def _():
        for t in range(NGLOB):
            wanted = gb_ref[t] - part * (2 * N)

            def look(slot, found):
                pick_k, pick_v = found
                keys, vals = kv[16 + slot, 0], kv[16 + slot, 1]
                for half in range(2):
                    here = wanted == 2 * slot + half
                    pick_k = jnp.where(here, keys[half * BLK : (half + 1) * BLK], pick_k)
                    pick_v = jnp.where(here, vals[half * BLK : (half + 1) * BLK], pick_v)
                return pick_k, pick_v

            zero = jnp.zeros((BLK, DH), jnp.bfloat16)
            pick_k, pick_v = lax.fori_loop(0, N, look, (zero, zero))
            g1src[2 * t] = pick_k
            g1src[2 * t + 1] = pick_v
        own_g1.start()

        for t in (4, 12, 3, 11, 5, 13, 2, 10, 6, 14, 1, 9, 7, 15, 8):
            g1_copy(lax.rem(part + t, N)).start()
        own_g1.wait()

    def wait_g1(source, _):
        @pl.when(source != part)
        def _():
            remote(
                g1src.at[0], g1buf.at[source], g1_send.at[0], g1_recv.at[source], (part, me)
            ).wait_recv()

        return 0

    lax.fori_loop(0, 4, wait_g1, 0)
    piece = jnp.zeros((BLK, DH), jnp.bfloat16)
    holder = gb_ref[part // 2] // (2 * N)
    for source in range(4):
        piece = jnp.where(holder == source, g1buf[source], piece)
    g2src[...] = piece

    ring = (part // 8) * 8
    opposite = lax.rem(part + 8, N)

    def g2_place(t):
        return gbuf.at[lax.rem(t, 2) * NGLOB + t // 2]

    def in_ring(step):
        return ring + lax.rem(part + step, 8)

    def g2_copy(slot, to):
        return remote(g2src, g2_place(slot), g2_send.at[to], g2_recv.at[slot], across(to))

    def g2_cross(slot):
        return remote(g2_place(slot), g2_place(slot), g2_over.at[slot], g2_recv.at[slot], across(opposite))

    own_g2 = pltpu.make_async_copy(g2src, g2_place(part), own_sem.at[1])
    own_g2.start()
    for step in FAR_FIRST:
        g2_copy(part, in_ring(step)).start()

    for dx, dc in MOVES[len(MOVES) - HELD :]:
        pl.when(part < 8)(functools.partial(forward, dx, dc))

    own_g2.wait()
    g2_cross(part).start()
    for step in reversed(FAR_FIRST):
        g2_copy(in_ring(step), part).wait_recv()
        g2_cross(in_ring(step)).start()

    own_q.wait()
    own_l.wait()

    def wait_q(t, _):
        slot = lax.rem(me + N - t, N)
        q_copy(slot, me).wait_recv()
        l_copy(slot, me).wait_recv()
        return 0

    lax.fori_loop(1, N, wait_q, 0)
    to_scalars = pltpu.make_async_copy(lbv, lbs, own_sem.at[2])
    to_scalars.start()
    to_scalars.wait()

    def wait_g2(t, _):
        g2_cross(8 - ring + t).wait_recv()
        return 0

    lax.fori_loop(0, 8, wait_g2, 0)

    def o_copy(group, source):
        columns = head_columns(out_ref, head_at(part, source))
        return remote(obuf.at[group], columns, o_send.at[group], o_recv.at[source], (part, group))

    own_o = pltpu.make_async_copy(obuf.at[me], head_columns(out_ref, head), own_sem.at[3])

    first = head_at(lax.rem(part + N - 1, N), head)

    def pair_low(n):
        dx = sum(jnp.where(n == at, 4 - move[0], 0) for at, move in enumerate(MOVES))
        dc = sum(jnp.where(n == at, move[1], 0) for at, move in enumerate(MOVES))
        low = moved(first, 0, dx, dc)
        return jnp.where(low >= 8, low - 8, low)

    def send_out(i):
        @pl.when(i == me)
        def _():
            own_o.start()

        @pl.when(i != me)
        def _():
            o_copy(i, me).start()

    def groups(masked_far, masked_glob):
        def step(n, _):
            upper = n < 4
            lows = [pair_low(2 * n + k - jnp.where(upper, 0, 8)) for k in range(2)]

            if not masked_far:

                @pl.when(upper)
                def _():
                    for low in lows:
                        halo_copy(low + 8).wait_recv()
                        halo_copy(low).wait_recv()

            two = [low + jnp.where(upper, 8, 0) for low in lows]
            made = [attend(part, i, masked_far, masked_glob, qbuf, kv, lbs, gb_ref, gbuf) for i in two]
            for i, rows in zip(two, made):
                obuf[i] = rows
            for i in two:
                send_out(i)
            return 0

        lax.fori_loop(0, 8, step, 0)

    @pl.when(part == 0)
    def _():
        groups(True, True)

    @pl.when((part > 0) & (part < 4))
    def _():
        groups(False, True)

    @pl.when(part >= 4)
    def _():
        groups(False, False)

    own_o.wait()

    def finish(t, _):
        other = lax.rem(me + t, N)
        k_copy(me, other).wait_send()
        v_copy(me, other).wait_send()
        q_copy(me, other).wait_send()
        l_copy(me, other).wait_send()
        o_copy(other, me).wait_send()
        o_copy(me, other).wait_recv()
        return 0

    lax.fori_loop(1, N, finish, 0)
    g2_cross(part).wait_send()
    for step in FAR_FIRST:
        g2_copy(part, in_ring(step)).wait_send()
        g2_cross(in_ring(step)).wait_send()

    @pl.when(part < N - 1)
    def _():
        def finish_halo(slot, _):
            halo_copy(slot).wait_send()
            return 0

        lax.fori_loop(0, N, finish_halo, 0)

    @pl.when(part < 4)
    def _():
        def finish_g1(t, _):
            g1_copy(lax.rem(part + t, N)).wait_send()
            return 0

        lax.fori_loop(1, N, finish_g1, 0)


def shards(queries, keys, values, level_blocks, global_blocks):
    rows, width = queries.shape
    anywhere = pl.BlockSpec(memory_space=pl.ANY)
    in_place = pl.BlockSpec(memory_space=pltpu.HBM)
    sems = pltpu.SemaphoreType.DMA
    return pl.pallas_call(
        kernel,
        out_shape=jax.ShapeDtypeStruct((rows, width), jnp.bfloat16),
        in_specs=[
            in_place,
            in_place,
            in_place,
            pl.BlockSpec(memory_space=pltpu.VMEM),
            pl.BlockSpec(memory_space=pltpu.SMEM),
        ],
        out_specs=anywhere,
        scratch_shapes=[
            pltpu.VMEM((N, GRP, DH), jnp.bfloat16),
            pltpu.VMEM((2 * N, 2, GRP, DH), jnp.bfloat16),
            pltpu.VMEM((N, 2, LEV), jnp.int32),
            pltpu.SMEM((N, 2, LEV), jnp.int32),
            pltpu.VMEM((N, BLK, DH), jnp.bfloat16),
            pltpu.VMEM((4, BLK, DH), jnp.bfloat16),
            pltpu.VMEM((BLK, DH), jnp.bfloat16),
            pltpu.VMEM((2 * NGLOB, BLK, DH), jnp.bfloat16),
            pltpu.VMEM((N, GRP, DH), jnp.bfloat16),
        ]
        + [sems((N,))] * 8
        + [sems((N,)), sems((N,)), sems((N,)), sems((4,)), sems((N,)), sems((N,)), sems((N,)), sems((N,)), sems((N,)), sems((4,))],
        compiler_params=pltpu.CompilerParams(
            collective_id=0, has_side_effects=True, vmem_limit_bytes=40 * 2**20
        ),
        cost_estimate=pl.CostEstimate(
            flops=4 * rows * width * 2048, bytes_accessed=8 * rows * width, transcendentals=rows * 2048 * N
        ),
    )(
        *[pltpu.with_memory_space_constraint(x, pltpu.HBM) for x in (queries, keys, values)],
        level_blocks,
        global_blocks,
    )


def solution(mesh):
    placed = P(("outer", "inner"), None)
    return jax.shard_map(
        shards,
        mesh=mesh,
        in_specs=(placed, placed, placed, placed, P()),
        out_specs=placed,
        check_vma=False,
    )
```
